512 devices in a mesh: group: 4 (over y), expert: 32 (over x_hi, z), tensor: 4 (over x_lo, core).
Axes of the slice: x: 4 (x_hi: 2, x_lo: 2; x = x_hi * 2 + x_lo), y: 4, z: 16, core: 2. Of those that a mesh axis runs over, the one named last changes fastest.
Arguments:
- weights: bfloat16 [32, 3584, 1024], P(None, ('group', 'expert'), 'tensor'), may hold values from -0.09375 to 0.09375
- gradients: bfloat16 [32, 3584, 1024], P(None, ('group', 'expert'), 'tensor'), may hold values from -6 to 6
- moment_one: float32 [32, 3584, 1024], P(None, ('group', 'expert'), 'tensor'), may hold values from -4 to 4
- moment_two: float32 [32, 3584, 1024], P(None, ('group', 'expert'), 'tensor'), may hold values from 0.1 to 4
- hidden_in: bfloat16 [4, 512, 3584], P(None, ('group', 'expert', 'tensor')), may hold values from -6 to 6
- query_latent: bfloat16 [4, 512, 16384], P(None, ('group', 'expert', 'tensor')), may hold values from -16 to 16
- query_rope: bfloat16 [4, 512, 2048], P(None, ('group', 'expert', 'tensor')), may hold values from -6 to 6
- cache_latent: bfloat16 [512, 256, 512], P(('group', 'expert', 'tensor')), may hold values from -8 to 8
- cache_rope: bfloat16 [512, 64, 256], P(('group', 'expert', 'tensor')), may hold values from -6 to 6
- new_latent: bfloat16 [4, 512, 512], P(None, ('group', 'expert', 'tensor')), may hold values from -6 to 6
- new_rope: bfloat16 [4, 512, 64], P(None, ('group', 'expert', 'tensor')), may hold values from -6 to 6
- lengths: int32 [512], P(('group', 'expert', 'tensor')), may hold values from 64 to 256, as said below
- expert_ids: int32 [4, 512, 8], P(None, ('group', 'expert')), may hold values from 0 to 31, all different within a row; in each aligned block of 4 rows (0 to 3, 4 to 7, ..., all dimensions but the last counted through in order) at most 2 rows name the same one
- router: bfloat16 [512, 32], replicated, may hold values from -0.5 to 0.5
Outputs:
- moment_one_new: float32 [32, 3584, 1024], P(None, ('group', 'expert'), 'tensor')
- moment_two_new: float32 [32, 3584, 1024], P(None, ('group', 'expert'), 'tensor')
- attention_out: bfloat16 [4, 512, 16384], P(None, ('group', 'expert', 'tensor'))
- expert_out: bfloat16 [4, 512, 1024], P(None, ('group', 'expert'), 'tensor')
The draws below stay inside these ranges and needn't reach their ends.
Inputs may be any that keep to these rules, and one draw needn't show every extreme that they name: `lengths`: each row holds between 64 and 256 filled slots; the first row holds 256. `expert_ids`: within a step, in each aligned block of 4 rows, no expert is chosen by more than 2 rows.
All inputs are finite; a program needn't handle non-finite values.
Results may differ from the reference program's by a relative error of at most 0.0059.
Values may be sent and summed in bfloat16 or wider, within the bound.
No kernel may reach another device: no remote copies, remote signals or barrier semaphores. Data moves between devices by JAX's collectives and lax.ppermute only.
A program may use at most 64 MiB of HBM per device.

```python
import math
import jax
import jax.numpy as jnp
import numpy as np
from jax import lax

D = 3584
FF = 1024
EXPERTS = 32
TOPK = 8
HEADS = 32
LAT = 512
ROPE = 64
STEPS = 4
LCACHE = 256
ROWS_DEV = 1
ROWS = 512
CAP = 2
N_TENSOR = 4


def draw_cache_latent(key, part):
    key = jax.random.fold_in(key, 5)
    values = jax.random.normal(key, (ROWS, LCACHE, LAT), jnp.float32)
    return jnp.clip(values, -7.5, 7.5).astype(jnp.bfloat16)


def draw_query_latent(key, part):
    key = jax.random.fold_in(key, 6)
    values = jax.random.normal(key, (STEPS, ROWS, HEADS, LAT), jnp.float32)
    values = jnp.clip(values, -6.0, 6.0)
    return values.reshape(STEPS, ROWS, HEADS * LAT).astype(jnp.bfloat16)


def draw_lengths(key, part):
    key = jax.random.fold_in(key, 7)
    filled = jax.random.randint(key, (ROWS,), LCACHE // 4, LCACHE + 1)
    return filled.at[0].set(LCACHE).astype(jnp.int32)


def shard_levels(rng, dims, pieces, low, high):
    gain = 1.0
    for position, blocks in pieces:
        steps = jax.random.uniform(jax.random.fold_in(jax.random.fold_in(rng, 6), position), (blocks,), jnp.float32, low / len(pieces), high / len(pieces))
        gain = gain * jnp.repeat(jnp.exp(steps), dims[position] // blocks).reshape((-1,) + (1,) * (len(dims) - 1 - position))
    return gain


def assign_block(stream_key, own, number, rows, count, top, limit, slope):
    ranking = jax.random.permutation(stream_key, count)
    crowded, usual = shares(count, rows * top, limit, slope, True), shares(count, rows * top, limit, slope, False)
    places = jnp.arange(count)

    def named(sizes, offset_by):
        used = int((sizes > 0).sum())
        fixed = max(1, used // 4)
        moved = fixed + (places - fixed + offset_by * (used - fixed)) % max(1, count - fixed)
        return jnp.zeros((count,), jnp.int32).at[ranking[jnp.where(places < fixed, places, moved)]].set(jnp.asarray(sizes, jnp.int32))

    sizes = jnp.where(number % 4 == 0, named(crowded, number // 4), named(usual, number - number // 4 - 1))
    mixed = jax.random.permutation(jax.random.fold_in(own, 3), count)
    giver, receiver = mixed[0:count // 2 * 2:2], mixed[1:count // 2 * 2:2]
    room = jnp.minimum(sizes[giver] - 1, limit - sizes[receiver]) // 2
    room = jnp.where((giver == ranking[0]) | (receiver == ranking[0]) | (sizes[receiver] == 0), 0, jnp.maximum(room, 0))
    moved = jax.random.randint(jax.random.fold_in(own, 4), (count // 2,), 0, 1 << 20) % (room + 1)
    sizes = sizes.at[giver].add(-moved).at[receiver].add(moved)
    members = jnp.searchsorted(jnp.cumsum(sizes), jnp.arange(rows * top), side="right").astype(jnp.int32)
    grid = members.reshape(top, rows).T
    grid = grid[jax.random.permutation(jax.random.fold_in(own, 1), rows)]
    offset_by = jax.random.randint(jax.random.fold_in(own, 2), (rows, 1), 0, top)
    return jnp.take_along_axis(grid, (jnp.arange(top)[None, :] + offset_by) % top, axis=1)


def shares(amount, total, limit, slope, full):
    weights = [(1 << 20) // math.isqrt(grade ** slope) + 1 for grade in range(1, amount + 1)]
    largest = limit if full else min(limit, max(-(-total // amount), total * weights[0] // sum(weights)))
    least = 1 if total - largest >= amount - 1 else 0
    given, spare = [largest] + [least] * (amount - 1), total - largest - least * (amount - 1)
    while spare > 0:
        candidates = [i for i in range(1, amount) if given[i] < largest] or [i for i in range(1, amount) if given[i] < limit]
        mass, remaining = sum([weights[i] for i in candidates]), spare
        for i in candidates:
            extra = min(limit - given[i], max(1, remaining * weights[i] // mass), spare)
            given[i] = given[i] + extra
            spare = spare - extra
    return np.array(given)


def gaussian(rng, shape, width, limit, shards=(), kind=jnp.bfloat16):
    drawn = jax.random.normal(rng, shape, jnp.float32) * width
    if len(shards) > 0:
        drawn = shard_levels(rng, shape, shards, -0.22, 0.18) * drawn
    return jnp.clip(drawn, min=-limit, max=limit).astype(kind)


def setup_inputs(seed: int = 0) -> dict:
    keys = jax.random.split(jax.random.key(seed), 15)
    weights = gaussian(keys[0], (EXPERTS, D, FF), D ** -0.5, 0.09375, ((1, 128), (2, 4)))
    gradients = gaussian(keys[1], (EXPERTS, D, FF), 1.0, 6.0, ((1, 128), (2, 4)))
    moment_one = gaussian(keys[2], (EXPERTS, D, FF), 0.5, 4.0, ((1, 128), (2, 4)), jnp.float32)
    moment_two = jnp.clip(jnp.exp(math.log(4.0) - 3.6888794 * jax.random.uniform(keys[3], (EXPERTS, D, FF), jnp.float32) ** shard_levels(keys[3], (EXPERTS, D, FF), ((1, 128), (2, 4)), -0.2, 0.2)), 0.1, 4.0)
    hidden_in = gaussian(keys[4], (STEPS, ROWS, D), 1.0, 6.0, ((1, 512),))
    query_latent = draw_query_latent(jax.random.fold_in(keys[14], 71), 0)
    query_rope = gaussian(keys[6], (STEPS, ROWS, HEADS * ROPE), 1.0, 6.0, ((1, 512),))
    cache_latent = draw_cache_latent(jax.random.fold_in(keys[14], 71), 0)
    cache_rope = gaussian(keys[8], (ROWS, ROPE, LCACHE), 1.0, 6.0, ((0, 512),))
    new_latent = gaussian(keys[9], (STEPS, ROWS, LAT), 1.0, 6.0, ((1, 512),))
    new_rope = gaussian(keys[10], (STEPS, ROWS, ROPE), 1.0, 6.0, ((1, 512),))
    lengths = draw_lengths(jax.random.fold_in(keys[14], 71), 0)
    expert_ids_keys = jax.random.split(jax.random.fold_in(keys[12], 1), STEPS * ROWS // (N_TENSOR * ROWS_DEV))
    expert_ids_turns = jax.random.permutation(jax.random.fold_in(keys[12], 3), STEPS * ROWS // (N_TENSOR * ROWS_DEV))
    expert_ids = jax.vmap(lambda own, number: assign_block(jax.random.fold_in(keys[12], 2), own, number, N_TENSOR * ROWS_DEV, EXPERTS, TOPK, CAP, 2))(expert_ids_keys, expert_ids_turns).reshape((STEPS, ROWS, TOPK))
    router = gaussian(keys[13], (LAT, EXPERTS), (LAT // 4) ** -0.5, 0.5)
    return dict(weights=weights, gradients=gradients, moment_one=moment_one, moment_two=moment_two, hidden_in=hidden_in, query_latent=query_latent, query_rope=query_rope, cache_latent=cache_latent, cache_rope=cache_rope, new_latent=new_latent, new_rope=new_rope, lengths=lengths, expert_ids=expert_ids, router=router)


BETA_ONE = 0.9
BETA_TWO = 0.95
LEARN_RATE = 0.005
WEIGHT_DECAY = 0.1
ADAM_EPS = 1e-08
BIAS_ONE = 1.0 - 0.9 ** 10
BIAS_TWO = 1.0 - 0.95 ** 10
QK_SCALE = 192.0 ** (-0.5)
ROUTE_SCALE = 2.827
NEGATIVE = -1e+30

def adamw(weights, gradients, moment_one, moment_two):
    grad_wide = gradients.astype(jnp.float32)
    first_new = BETA_ONE * moment_one + (1.0 - BETA_ONE) * grad_wide
    second_new = BETA_TWO * moment_two + (1.0 - BETA_TWO) * grad_wide * grad_wide
    old_weight = weights.astype(jnp.float32)
    ratio = first_new / BIAS_ONE / (jnp.sqrt(second_new / BIAS_TWO) + ADAM_EPS)
    updated = (old_weight - LEARN_RATE * (ratio + WEIGHT_DECAY * old_weight)).astype(jnp.bfloat16)
    return (first_new, second_new, updated)

def attend(query_latent, query_rope, cache_latent, cache_rope, new_latent, new_rope, lengths):
    step_count, row_count = (query_latent.shape[0], query_latent.shape[1])
    query_lat = query_latent.astype(jnp.float32).reshape(step_count, row_count, HEADS, LAT)
    query_pos = query_rope.astype(jnp.float32).reshape(step_count, row_count, HEADS, ROPE)
    cache_lat = cache_latent.astype(jnp.float32)
    fresh_lat = new_latent.astype(jnp.float32)
    old_scores = (jnp.einsum('srhc,rlc->srhl', query_lat, cache_lat) + jnp.einsum('srhp,rpl->srhl', query_pos, cache_rope.astype(jnp.float32))) * QK_SCALE
    new_scores = (jnp.einsum('srhc,trc->srht', query_lat, fresh_lat) + jnp.einsum('srhp,trp->srht', query_pos, new_rope.astype(jnp.float32))) * QK_SCALE
    valid_old = jnp.arange(LCACHE, dtype=jnp.int32)[None, :] < lengths[:, None]
    valid_new = jnp.arange(STEPS)[None, :] <= jnp.arange(STEPS)[:, None]
    old_scores = jnp.where(valid_old[None, :, None, :], old_scores, NEGATIVE)
    new_scores = jnp.where(valid_new[:, None, None, :], new_scores, NEGATIVE)
    peak_score = jnp.maximum(lax.optimization_barrier(jnp.max(old_scores, -1, keepdims=True)), lax.optimization_barrier(jnp.max(new_scores, -1, keepdims=True)))
    old_mass = jnp.exp(old_scores - peak_score)
    new_mass = jnp.exp(new_scores - peak_score)
    total_mass = lax.optimization_barrier(jnp.sum(old_mass, -1, keepdims=True)) + lax.optimization_barrier(jnp.sum(new_mass, -1, keepdims=True))
    old_prob = (old_mass / total_mass).astype(jnp.bfloat16)
    new_prob = (new_mass / total_mass).astype(jnp.bfloat16)
    mixture = jnp.einsum('srhl,rlc->srhc', old_prob.astype(jnp.float32), cache_lat) + jnp.einsum('srht,trc->srhc', new_prob.astype(jnp.float32), fresh_lat)
    summary = lax.optimization_barrier(jnp.mean(mixture, 2))
    summary = summary * lax.rsqrt(lax.optimization_barrier(jnp.mean(summary * summary, -1, keepdims=True)) + 1e-05)
    attention_out = mixture.reshape(step_count, row_count, HEADS * LAT).astype(jnp.bfloat16)
    return (attention_out, summary.astype(jnp.bfloat16))

def reference(weights, gradients, moment_one, moment_two, hidden_in, query_latent, query_rope, cache_latent, cache_rope, new_latent, new_rope, lengths, expert_ids, router):
    first_new, second_new, updated = adamw(weights, gradients, moment_one, moment_two)
    attention_out, summary = attend(query_latent, query_rope, cache_latent, cache_rope, new_latent, new_rope, lengths)
    logits = jnp.dot(summary.reshape(STEPS * ROWS, LAT), router, preferred_element_type=jnp.float32)
    gate_prob = jax.nn.sigmoid(logits)
    flat_ids = expert_ids.reshape(STEPS * ROWS, TOPK)
    chosen = jnp.take_along_axis(gate_prob, flat_ids, axis=1)
    route_weight = (ROUTE_SCALE * chosen / lax.optimization_barrier(jnp.sum(chosen, -1, keepdims=True))).astype(jnp.bfloat16)
    flat_rows = hidden_in.reshape(STEPS * ROWS, D)

    def one_expert(running, index):
        active = jax.nn.silu(jnp.dot(flat_rows, updated[index], preferred_element_type=jnp.float32)).astype(jnp.bfloat16)
        share = lax.optimization_barrier(jnp.sum(jnp.where(flat_ids == index, route_weight.astype(jnp.float32), 0.0), -1))
        return (running + share[:, None] * active.astype(jnp.float32), None)
    running, unused = lax.scan(one_expert, jnp.zeros((STEPS * ROWS, FF), jnp.float32), jnp.arange(EXPERTS, dtype=jnp.int32))
    expert_out = running.reshape(STEPS, ROWS, FF).astype(jnp.bfloat16)
    return (first_new, second_new, attention_out, expert_out)
```

```python
import jax
import jax.numpy as jnp
from jax import lax
from jax.sharding import PartitionSpec as P

EXPERTS = 32
HEADS = 32
LAT = 512
ROPE = 64


BETA_ONE = 0.9
BETA_TWO = 0.95
LEARN_RATE = 0.005
WEIGHT_DECAY = 0.1
ADAM_EPS = 1e-08
BIAS_ONE = 1.0 - 0.9**10
BIAS_TWO = 1.0 - 0.95**10
QK_SCALE = 192.0 ** (-0.5)
ROUTE_SCALE = 2.827
NEGATIVE = -1e30


def adamw(weights, gradients, moment_one, moment_two):
    grad_wide = gradients.astype(jnp.float32)
    first_new = BETA_ONE * moment_one + (1.0 - BETA_ONE) * grad_wide
    second_new = BETA_TWO * moment_two + (1.0 - BETA_TWO) * grad_wide * grad_wide
    old_weight = weights.astype(jnp.float32)
    ratio = first_new / BIAS_ONE / (jnp.sqrt(second_new / BIAS_TWO) + ADAM_EPS)
    updated = (old_weight - LEARN_RATE * (ratio + WEIGHT_DECAY * old_weight)).astype(jnp.bfloat16)
    return (first_new, second_new, updated)


def attend(query_latent, query_rope, cache_latent, cache_rope, new_latent, new_rope, lengths):
    step_count, row_count = (query_latent.shape[0], query_latent.shape[1])
    slot_total = cache_latent.shape[1]
    query_lat = query_latent.reshape(step_count, row_count, HEADS, LAT)
    query_pos = query_rope.reshape(step_count, row_count, HEADS, ROPE)
    old_scores = (
        jnp.einsum("srhc,rlc->srhl", query_lat, cache_latent, preferred_element_type=jnp.float32)
        + jnp.einsum("srhp,rpl->srhl", query_pos, cache_rope, preferred_element_type=jnp.float32)
    ) * QK_SCALE
    new_scores = (
        jnp.einsum("srhc,trc->srht", query_lat, new_latent, preferred_element_type=jnp.float32)
        + jnp.einsum("srhp,trp->srht", query_pos, new_rope, preferred_element_type=jnp.float32)
    ) * QK_SCALE
    valid_old = jnp.arange(slot_total, dtype=jnp.int32)[None, :] < lengths[:, None]
    valid_new = jnp.arange(step_count)[None, :] <= jnp.arange(step_count)[:, None]
    old_scores = jnp.where(valid_old[None, :, None, :], old_scores, NEGATIVE)
    new_scores = jnp.where(valid_new[:, None, None, :], new_scores, NEGATIVE)
    peak_score = jnp.maximum(
        jnp.max(old_scores, -1, keepdims=True), jnp.max(new_scores, -1, keepdims=True)
    )
    old_mass = jnp.exp(old_scores - peak_score)
    new_mass = jnp.exp(new_scores - peak_score)
    total_mass = jnp.sum(old_mass, -1, keepdims=True) + jnp.sum(new_mass, -1, keepdims=True)
    old_prob = (old_mass / total_mass).astype(jnp.bfloat16)
    new_prob = (new_mass / total_mass).astype(jnp.bfloat16)
    mixture = jnp.einsum(
        "srhl,rlc->srhc", old_prob, cache_latent, preferred_element_type=jnp.float32
    ) + jnp.einsum("srht,trc->srhc", new_prob, new_latent, preferred_element_type=jnp.float32)
    summary = jnp.mean(mixture, 2)
    summary = summary * lax.rsqrt(jnp.mean(summary * summary, -1, keepdims=True) + 1e-05)
    attention_out = mixture.reshape(step_count, row_count, HEADS * LAT).astype(jnp.bfloat16)
    return (attention_out, summary.astype(jnp.bfloat16))


def flip(value, axis, distance):
    size = lax.axis_size(axis)
    return lax.ppermute(value, axis, [(i, i ^ distance) for i in range(size)])


def local(
    weights,
    gradients,
    moment_one,
    moment_two,
    hidden_in,
    query_latent,
    query_rope,
    cache_latent,
    cache_rope,
    new_latent,
    new_rope,
    lengths,
    expert_ids,
    router,
):
    first_new, second_new, updated = adamw(weights, gradients, moment_one, moment_two)
    expert_count, slab, columns = updated.shape
    attention_out, summary = attend(
        query_latent, query_rope, cache_latent, cache_rope, new_latent, new_rope, lengths
    )
    step_count, _, width = hidden_in.shape
    quarter = width // 4
    group, tensor = lax.axis_index("group"), lax.axis_index("tensor")
    rows_all = lax.all_gather(hidden_in, "tensor", axis=1, tiled=True)
    block_rows = rows_all.shape[1]
    slot_count = 2
    places = step_count * slot_count

    picked = (expert_ids[..., None] == jnp.arange(EXPERTS, dtype=jnp.int32)).astype(jnp.float32)
    per_expert = jnp.sum(picked, 2)
    earlier = jnp.cumsum(per_expert, 1) - per_expert
    slot_hit = (earlier[..., None] == jnp.arange(slot_count, dtype=jnp.float32)).astype(
        jnp.float32
    ) * per_expert[..., None]
    my_part = lax.dynamic_slice_in_dim(rows_all, tensor * quarter, quarter, 2)
    outgoing = jnp.einsum(
        "sbec,sbd->escd",
        slot_hit.astype(jnp.bfloat16),
        my_part,
        preferred_element_type=jnp.float32,
    ).astype(jnp.bfloat16)
    outgoing = outgoing.reshape(expert_count, places * quarter // 128, 128)
    slabs = jnp.swapaxes(updated.reshape(expert_count, slab, 2, 128), 1, 2)
    slabs = slabs.reshape(expert_count, 2 * slab, 128)
    payload = jnp.concatenate([slabs, outgoing], 1)
    arrived = lax.all_to_all(payload, "expert", split_axis=0, concat_axis=0, tiled=True)
    held = jnp.swapaxes(arrived[:, : 2 * slab].reshape(expert_count, 2, slab, 128), 1, 2)
    held = held.reshape(expert_count * slab, columns)
    rows_in = arrived[:, 2 * slab :].reshape(expert_count * places, quarter)

    held_other = [flip(held, "group", k) for k in (1, 3, 2)]
    rows_far = flip(rows_in, "tensor", 2)
    rows_core = flip(rows_in, "tensor", 1)
    rows_diag = flip(rows_far, "tensor", 1)

    summary_all = lax.all_gather(summary, "tensor", axis=1, tiled=True)
    logits = jnp.einsum("sbc,ce->sbe", summary_all, router, preferred_element_type=jnp.float32)
    gate_prob = jax.nn.sigmoid(logits)
    chosen = jnp.sum(picked * gate_prob[:, :, None, :], -1)
    route_weight = (ROUTE_SCALE * chosen / jnp.sum(chosen, -1, keepdims=True)).astype(jnp.bfloat16)
    expert_weight = jnp.sum(picked * route_weight.astype(jnp.float32)[..., None], 2)
    combine = (slot_hit * expert_weight[..., None]).astype(jnp.bfloat16)

    rows_stack = jnp.stack([rows_in, rows_core, rows_far, rows_diag])
    turn = jnp.bitwise_xor(group, tensor)
    pre_act = jnp.zeros((expert_count * places, columns), jnp.float32)
    for k, piece in zip((0, 1, 3, 2), [held] + held_other):
        part = lax.dynamic_index_in_dim(rows_stack, jnp.bitwise_xor(turn, k), 0, keepdims=False)
        pre_act = pre_act + jnp.dot(part, piece, preferred_element_type=jnp.float32)
    active = jax.nn.silu(pre_act).astype(jnp.bfloat16)
    active = active.reshape(expert_count, places, columns)
    returned = lax.all_to_all(active, "expert", split_axis=0, concat_axis=0, tiled=True)
    returned = returned.reshape(EXPERTS, step_count, slot_count, columns)
    expert_out = jnp.einsum(
        "sbec,escf->sbf", combine, returned, preferred_element_type=jnp.float32
    ).astype(jnp.bfloat16)
    return (first_new, second_new, attention_out, expert_out)


def solution(mesh):
    return jax.shard_map(
        local,
        mesh=mesh,
        in_specs=(
            P(None, ("group", "expert"), "tensor"),
            P(None, ("group", "expert"), "tensor"),
            P(None, ("group", "expert"), "tensor"),
            P(None, ("group", "expert"), "tensor"),
            P(None, ("group", "expert", "tensor"), None),
            P(None, ("group", "expert", "tensor"), None),
            P(None, ("group", "expert", "tensor"), None),
            P(("group", "expert", "tensor"), None, None),
            P(("group", "expert", "tensor"), None, None),
            P(None, ("group", "expert", "tensor"), None),
            P(None, ("group", "expert", "tensor"), None),
            P(("group", "expert", "tensor")),
            P(None, ("group", "expert"), None),
            P(),
        ),
        out_specs=(
            P(None, ("group", "expert"), "tensor"),
            P(None, ("group", "expert"), "tensor"),
            P(None, ("group", "expert", "tensor"), None),
            P(None, ("group", "expert"), "tensor"),
        ),
        check_vma=False,
    )
```

```python
import jax
import jax.numpy as jnp
from jax import lax
from jax.sharding import PartitionSpec as P

EXPERTS = 32
HEADS = 32
LAT = 512
ROPE = 64


BETA_ONE = 0.9
BETA_TWO = 0.95
LEARN_RATE = 0.005
WEIGHT_DECAY = 0.1
ADAM_EPS = 1e-08
BIAS_ONE = 1.0 - 0.9**10
BIAS_TWO = 1.0 - 0.95**10
QK_SCALE = 192.0 ** (-0.5)
ROUTE_SCALE = 2.827
NEGATIVE = -1e30


def adamw(weights, gradients, moment_one, moment_two):
    grad_wide = gradients.astype(jnp.float32)
    first_new = BETA_ONE * moment_one + (1.0 - BETA_ONE) * grad_wide
    second_new = BETA_TWO * moment_two + (1.0 - BETA_TWO) * grad_wide * grad_wide
    old_weight = weights.astype(jnp.float32)
    ratio = first_new / BIAS_ONE / (jnp.sqrt(second_new / BIAS_TWO) + ADAM_EPS)
    updated = (old_weight - LEARN_RATE * (ratio + WEIGHT_DECAY * old_weight)).astype(jnp.bfloat16)
    return (first_new, second_new, updated)


def attend(query_latent, query_rope, cache_latent, cache_rope, new_latent, new_rope, lengths):
    step_count, row_count = (query_latent.shape[0], query_latent.shape[1])
    slot_total = cache_latent.shape[1]
    query_lat = query_latent.reshape(step_count, row_count, HEADS, LAT)
    query_pos = query_rope.reshape(step_count, row_count, HEADS, ROPE)
    old_scores = (
        jnp.einsum("srhc,rlc->srhl", query_lat, cache_latent, preferred_element_type=jnp.float32)
        + jnp.einsum("srhp,rpl->srhl", query_pos, cache_rope, preferred_element_type=jnp.float32)
    ) * QK_SCALE
    new_scores = (
        jnp.einsum("srhc,trc->srht", query_lat, new_latent, preferred_element_type=jnp.float32)
        + jnp.einsum("srhp,trp->srht", query_pos, new_rope, preferred_element_type=jnp.float32)
    ) * QK_SCALE
    valid_old = jnp.arange(slot_total, dtype=jnp.int32)[None, :] < lengths[:, None]
    valid_new = jnp.arange(step_count)[None, :] <= jnp.arange(step_count)[:, None]
    old_scores = jnp.where(valid_old[None, :, None, :], old_scores, NEGATIVE)
    new_scores = jnp.where(valid_new[:, None, None, :], new_scores, NEGATIVE)
    peak_score = jnp.maximum(
        jnp.max(old_scores, -1, keepdims=True), jnp.max(new_scores, -1, keepdims=True)
    )
    old_mass = jnp.exp(old_scores - peak_score)
    new_mass = jnp.exp(new_scores - peak_score)
    total_mass = jnp.sum(old_mass, -1, keepdims=True) + jnp.sum(new_mass, -1, keepdims=True)
    old_prob = (old_mass / total_mass).astype(jnp.bfloat16)
    new_prob = (new_mass / total_mass).astype(jnp.bfloat16)
    mixture = jnp.einsum(
        "srhl,rlc->srhc", old_prob, cache_latent, preferred_element_type=jnp.float32
    ) + jnp.einsum("srht,trc->srhc", new_prob, new_latent, preferred_element_type=jnp.float32)
    summary = jnp.mean(mixture, 2)
    summary = summary * lax.rsqrt(jnp.mean(summary * summary, -1, keepdims=True) + 1e-05)
    attention_out = mixture.reshape(step_count, row_count, HEADS * LAT).astype(jnp.bfloat16)
    return (attention_out, summary.astype(jnp.bfloat16))


def flip(value, axis, distance):
    size = lax.axis_size(axis)
    return lax.ppermute(value, axis, [(i, i ^ distance) for i in range(size)])


def local(
    weights,
    gradients,
    moment_one,
    moment_two,
    hidden_in,
    query_latent,
    query_rope,
    cache_latent,
    cache_rope,
    new_latent,
    new_rope,
    lengths,
    expert_ids,
    router,
):
    first_new, second_new, updated = adamw(weights, gradients, moment_one, moment_two)
    expert_count, slab, columns = updated.shape
    step_count, _, width = hidden_in.shape
    quarter = width // 4
    tensor = lax.axis_index("tensor")
    rows_all = lax.all_gather(hidden_in, "tensor", axis=1, tiled=True)
    block_rows = rows_all.shape[1]
    slot_count = 2
    places = step_count * slot_count

    picked = (expert_ids[..., None] == jnp.arange(EXPERTS, dtype=jnp.int32)).astype(jnp.float32)
    per_expert = jnp.sum(picked, 2)
    earlier = jnp.cumsum(per_expert, 1) - per_expert
    slot_hit = (earlier[..., None] == jnp.arange(slot_count, dtype=jnp.float32)).astype(
        jnp.float32
    ) * per_expert[..., None]
    my_part = lax.dynamic_slice_in_dim(rows_all, tensor * quarter, quarter, 2)
    outgoing = jnp.einsum(
        "sbec,sbd->escd",
        slot_hit.astype(jnp.bfloat16),
        my_part,
        preferred_element_type=jnp.float32,
    ).astype(jnp.bfloat16)
    outgoing = outgoing.reshape(expert_count, places * quarter // 128, 128)
    slabs = jnp.swapaxes(updated.reshape(expert_count, slab, 2, 128), 1, 2)
    slabs = slabs.reshape(expert_count, 2 * slab, 128)
    payload = jnp.concatenate([slabs, outgoing], 1)
    payload, query_latent, query_rope, new_latent, new_rope = lax.optimization_barrier(
        (payload, query_latent, query_rope, new_latent, new_rope)
    )
    attention_out, summary = attend(
        query_latent, query_rope, cache_latent, cache_rope, new_latent, new_rope, lengths
    )
    arrived = lax.all_to_all(payload, "expert", split_axis=0, concat_axis=0, tiled=True)
    held = jnp.swapaxes(arrived[:, : 2 * slab].reshape(expert_count, 2, slab, 128), 1, 2)
    held = held.reshape(expert_count * slab, columns)
    rows_in = arrived[:, 2 * slab :].reshape(expert_count * places, quarter)

    copies = jnp.broadcast_to(held[None], (lax.axis_size("group"),) + held.shape)
    whole = lax.all_to_all(copies, "group", split_axis=0, concat_axis=0, tiled=True)
    rows_far = flip(rows_in, "tensor", 2)
    rows_core = flip(rows_in, "tensor", 1)
    rows_diag = flip(rows_far, "tensor", 1)

    summary_all = lax.all_gather(summary, "tensor", axis=1, tiled=True)
    logits = jnp.einsum("sbc,ce->sbe", summary_all, router, preferred_element_type=jnp.float32)
    gate_prob = jax.nn.sigmoid(logits)
    chosen = jnp.sum(picked * gate_prob[:, :, None, :], -1)
    route_weight = (ROUTE_SCALE * chosen / jnp.sum(chosen, -1, keepdims=True)).astype(jnp.bfloat16)
    expert_weight = jnp.sum(picked * route_weight.astype(jnp.float32)[..., None], 2)
    combine = (slot_hit * expert_weight[..., None]).astype(jnp.bfloat16)

    pre_act = jnp.zeros((expert_count * places, columns), jnp.float32)
    for k, part in enumerate((rows_in, rows_core, rows_far, rows_diag)):
        piece = lax.dynamic_index_in_dim(whole, jnp.bitwise_xor(tensor, k), 0, keepdims=False)
        pre_act = pre_act + jnp.dot(part, piece, preferred_element_type=jnp.float32)
    active = jax.nn.silu(pre_act).astype(jnp.bfloat16)
    active = active.reshape(expert_count, places, columns)
    returned = lax.all_to_all(active, "expert", split_axis=0, concat_axis=0, tiled=True)
    returned = returned.reshape(EXPERTS, step_count, slot_count, columns)
    expert_out = jnp.einsum(
        "sbec,escf->sbf", combine, returned, preferred_element_type=jnp.float32
    ).astype(jnp.bfloat16)
    return (first_new, second_new, attention_out, expert_out)


def solution(mesh):
    return jax.shard_map(
        local,
        mesh=mesh,
        in_specs=(
            P(None, ("group", "expert"), "tensor"),
            P(None, ("group", "expert"), "tensor"),
            P(None, ("group", "expert"), "tensor"),
            P(None, ("group", "expert"), "tensor"),
            P(None, ("group", "expert", "tensor"), None),
            P(None, ("group", "expert", "tensor"), None),
            P(None, ("group", "expert", "tensor"), None),
            P(("group", "expert", "tensor"), None, None),
            P(("group", "expert", "tensor"), None, None),
            P(None, ("group", "expert", "tensor"), None),
            P(None, ("group", "expert", "tensor"), None),
            P(("group", "expert", "tensor")),
            P(None, ("group", "expert"), None),
            P(),
        ),
        out_specs=(
            P(None, ("group", "expert"), "tensor"),
            P(None, ("group", "expert"), "tensor"),
            P(None, ("group", "expert", "tensor"), None),
            P(None, ("group", "expert"), "tensor"),
        ),
        check_vma=False,
    )
```

```python
import jax
import jax.numpy as jnp
from jax import lax
from jax.sharding import PartitionSpec as P

EXPERTS = 32
HEADS = 32
LAT = 512
ROPE = 64
RING = 16


BETA_ONE = 0.9
BETA_TWO = 0.95
LEARN_RATE = 0.005
WEIGHT_DECAY = 0.1
ADAM_EPS = 1e-08
BIAS_ONE = 1.0 - 0.9**10
BIAS_TWO = 1.0 - 0.95**10
QK_SCALE = 192.0 ** (-0.5)
ROUTE_SCALE = 2.827
NEGATIVE = -1e30


def adamw(weights, gradients, moment_one, moment_two):
    grad_wide = gradients.astype(jnp.float32)
    first_new = BETA_ONE * moment_one + (1.0 - BETA_ONE) * grad_wide
    second_new = BETA_TWO * moment_two + (1.0 - BETA_TWO) * grad_wide * grad_wide
    old_weight = weights.astype(jnp.float32)
    ratio = first_new / BIAS_ONE / (jnp.sqrt(second_new / BIAS_TWO) + ADAM_EPS)
    updated = (old_weight - LEARN_RATE * (ratio + WEIGHT_DECAY * old_weight)).astype(jnp.bfloat16)
    return (first_new, second_new, updated)


def attend(query_latent, query_rope, cache_latent, cache_rope, new_latent, new_rope, lengths):
    step_count, row_count = (query_latent.shape[0], query_latent.shape[1])
    slot_total = cache_latent.shape[1]
    query_lat = query_latent.reshape(step_count, row_count, HEADS, LAT)
    query_pos = query_rope.reshape(step_count, row_count, HEADS, ROPE)
    old_scores = (
        jnp.einsum("srhc,rlc->srhl", query_lat, cache_latent, preferred_element_type=jnp.float32)
        + jnp.einsum("srhp,rpl->srhl", query_pos, cache_rope, preferred_element_type=jnp.float32)
    ) * QK_SCALE
    new_scores = (
        jnp.einsum("srhc,trc->srht", query_lat, new_latent, preferred_element_type=jnp.float32)
        + jnp.einsum("srhp,trp->srht", query_pos, new_rope, preferred_element_type=jnp.float32)
    ) * QK_SCALE
    valid_old = jnp.arange(slot_total, dtype=jnp.int32)[None, :] < lengths[:, None]
    valid_new = jnp.arange(step_count)[None, :] <= jnp.arange(step_count)[:, None]
    old_scores = jnp.where(valid_old[None, :, None, :], old_scores, NEGATIVE)
    new_scores = jnp.where(valid_new[:, None, None, :], new_scores, NEGATIVE)
    peak_score = jnp.maximum(
        jnp.max(old_scores, -1, keepdims=True), jnp.max(new_scores, -1, keepdims=True)
    )
    old_mass = jnp.exp(old_scores - peak_score)
    new_mass = jnp.exp(new_scores - peak_score)
    total_mass = jnp.sum(old_mass, -1, keepdims=True) + jnp.sum(new_mass, -1, keepdims=True)
    old_prob = (old_mass / total_mass).astype(jnp.bfloat16)
    new_prob = (new_mass / total_mass).astype(jnp.bfloat16)
    mixture = jnp.einsum(
        "srhl,rlc->srhc", old_prob, cache_latent, preferred_element_type=jnp.float32
    ) + jnp.einsum("srht,trc->srhc", new_prob, new_latent, preferred_element_type=jnp.float32)
    summary = jnp.mean(mixture, 2)
    summary = summary * lax.rsqrt(jnp.mean(summary * summary, -1, keepdims=True) + 1e-05)
    attention_out = mixture.reshape(step_count, row_count, HEADS * LAT).astype(jnp.bfloat16)
    return (attention_out, summary.astype(jnp.bfloat16))


def shift(value, distance):
    pairs = [
        (x * RING + (z + distance) % RING, x * RING + z) for x in range(2) for z in range(RING)
    ]
    return lax.ppermute(value, "expert", pairs)


def flip(value, axis, distance):
    size = lax.axis_size(axis)
    return lax.ppermute(value, axis, [(i, i ^ distance) for i in range(size)])


def local(
    weights,
    gradients,
    moment_one,
    moment_two,
    hidden_in,
    query_latent,
    query_rope,
    cache_latent,
    cache_rope,
    new_latent,
    new_rope,
    lengths,
    expert_ids,
    router,
):
    step_count, _, width = hidden_in.shape
    quarter = width // 4
    top_count = expert_ids.shape[2]
    expert, tensor = lax.axis_index("expert"), lax.axis_index("tensor")
    side, ring = expert // RING, expert % RING
    slot_count = 2
    places = step_count * slot_count

    own_ids = lax.dynamic_index_in_dim(expert_ids, tensor, 1, keepdims=False)
    own_ids = jnp.pad(own_ids.astype(jnp.bfloat16), ((0, 0), (0, 128 - top_count)))
    parts = jnp.swapaxes(hidden_in.reshape(step_count, 4, quarter), 0, 1)
    parts = jnp.concatenate([parts, jnp.broadcast_to(own_ids, (4,) + own_ids.shape)], -1)
    parts = jnp.broadcast_to(parts[None], (4,) + parts.shape).reshape((16,) + parts.shape[1:])
    parts, query_latent, query_rope, new_latent, new_rope = lax.optimization_barrier(
        (parts, query_latent, query_rope, new_latent, new_rope)
    )
    far_groups = [
        [(x * RING + 4 * b + r) * 4 + t for b in range(4) for t in range(4)]
        for x in range(2)
        for r in range(4)
    ]
    near = lax.all_to_all(
        parts,
        ("expert", "tensor"),
        split_axis=0,
        concat_axis=0,
        tiled=True,
        axis_index_groups=far_groups,
    )

    first_new, second_new, updated = adamw(weights, gradients, moment_one, moment_two)
    expert_count, slab, columns = updated.shape
    attention_out, summary = attend(
        query_latent, query_rope, cache_latent, cache_rope, new_latent, new_rope, lengths
    )

    near, updated = lax.optimization_barrier((near, updated))
    held = lax.all_to_all(updated, "expert", split_axis=0, concat_axis=0, tiled=True)
    held = held.reshape(expert_count * slab, columns)

    both = jnp.stack([near, flip(near, "expert", RING)])
    pieces = [both] + [shift(both, j) for j in (1, 2, -1)]
    pieces = jnp.stack(pieces).reshape((8, 4, 4, step_count, quarter + 128))
    order = [
        lax.rem(r + 4 - lax.rem(ring, 4), 4) * 2 + jnp.bitwise_xor(x, side)
        for x in range(2)
        for r in range(4)
    ]
    rows_all = jnp.stack([lax.dynamic_index_in_dim(pieces, i, 0, keepdims=False) for i in order])
    rows_all = rows_all.reshape(2, 4, 4, 4, step_count, quarter + 128)
    ids = rows_all[..., quarter : quarter + top_count]
    wanted = jnp.sum((ids == expert.astype(jnp.bfloat16)).astype(jnp.float32), -1)
    before = jnp.cumsum(wanted, 3) - wanted
    chosen_rows = []
    for c in range(slot_count):
        take = wanted * (before == c).astype(jnp.float32)
        chosen_rows.append(
            jnp.sum(take[..., None] * rows_all[..., :quarter].astype(jnp.float32), 3)
        )
    rows_in = jnp.stack(chosen_rows, 3).astype(jnp.bfloat16)
    rows_in = jnp.transpose(rows_in, (0, 2, 1, 3, 4, 5)).reshape(expert_count * places, quarter)

    copies = jnp.broadcast_to(held[None], (lax.axis_size("group"),) + held.shape)
    whole = lax.all_to_all(copies, "group", split_axis=0, concat_axis=0, tiled=True)
    rows_far = flip(rows_in, "tensor", 2)
    rows_core = flip(rows_in, "tensor", 1)
    rows_diag = flip(rows_far, "tensor", 1)

    summary_all = lax.all_gather(summary, "tensor", axis=1, tiled=True)
    logits = jnp.einsum("sbc,ce->sbe", summary_all, router, preferred_element_type=jnp.float32)
    gate_prob = jax.nn.sigmoid(logits)
    picked = (expert_ids[..., None] == jnp.arange(EXPERTS, dtype=jnp.int32)).astype(jnp.float32)
    per_expert = jnp.sum(picked, 2)
    earlier = jnp.cumsum(per_expert, 1) - per_expert
    slot_hit = (earlier[..., None] == jnp.arange(slot_count, dtype=jnp.float32)).astype(
        jnp.float32
    ) * per_expert[..., None]
    chosen = jnp.sum(picked * gate_prob[:, :, None, :], -1)
    route_weight = (ROUTE_SCALE * chosen / jnp.sum(chosen, -1, keepdims=True)).astype(jnp.bfloat16)
    expert_weight = jnp.sum(picked * route_weight.astype(jnp.float32)[..., None], 2)
    combine = (slot_hit * expert_weight[..., None]).astype(jnp.bfloat16)

    pre_act = jnp.zeros((expert_count * places, columns), jnp.float32)
    for k, part in enumerate((rows_in, rows_core, rows_far, rows_diag)):
        piece = lax.dynamic_index_in_dim(whole, jnp.bitwise_xor(tensor, k), 0, keepdims=False)
        pre_act = pre_act + jnp.dot(part, piece, preferred_element_type=jnp.float32)
    active = jax.nn.silu(pre_act).astype(jnp.bfloat16)
    active = active.reshape(expert_count, places, columns)
    returned = lax.all_to_all(active, "expert", split_axis=0, concat_axis=0, tiled=True)
    returned = returned.reshape(EXPERTS, slot_count, step_count, columns)
    expert_out = jnp.einsum(
        "sbec,ecsf->sbf", combine, returned, preferred_element_type=jnp.float32
    ).astype(jnp.bfloat16)
    return (first_new, second_new, attention_out, expert_out)


def solution(mesh):
    return jax.shard_map(
        local,
        mesh=mesh,
        in_specs=(
            P(None, ("group", "expert"), "tensor"),
            P(None, ("group", "expert"), "tensor"),
            P(None, ("group", "expert"), "tensor"),
            P(None, ("group", "expert"), "tensor"),
            P(None, ("group", "expert", "tensor"), None),
            P(None, ("group", "expert", "tensor"), None),
            P(None, ("group", "expert", "tensor"), None),
            P(("group", "expert", "tensor"), None, None),
            P(("group", "expert", "tensor"), None, None),
            P(None, ("group", "expert", "tensor"), None),
            P(None, ("group", "expert", "tensor"), None),
            P(("group", "expert", "tensor")),
            P(None, ("group", "expert"), None),
            P(),
        ),
        out_specs=(
            P(None, ("group", "expert"), "tensor"),
            P(None, ("group", "expert"), "tensor"),
            P(None, ("group", "expert", "tensor"), None),
            P(None, ("group", "expert"), "tensor"),
        ),
        check_vma=False,
    )
```

```python
import jax
import jax.numpy as jnp
from jax import lax
from jax.sharding import PartitionSpec as P

EXPERTS = 32
HEADS = 32
LAT = 512
ROPE = 64


BETA_ONE = 0.9
BETA_TWO = 0.95
LEARN_RATE = 0.005
WEIGHT_DECAY = 0.1
ADAM_EPS = 1e-08
BIAS_ONE = 1.0 - 0.9**10
BIAS_TWO = 1.0 - 0.95**10
QK_SCALE = 192.0 ** (-0.5)
ROUTE_SCALE = 2.827
NEGATIVE = -1e30


def adamw(weights, gradients, moment_one, moment_two):
    grad_wide = gradients.astype(jnp.float32)
    first_new = BETA_ONE * moment_one + (1.0 - BETA_ONE) * grad_wide
    second_new = BETA_TWO * moment_two + (1.0 - BETA_TWO) * grad_wide * grad_wide
    old_weight = weights.astype(jnp.float32)
    ratio = first_new / BIAS_ONE / (jnp.sqrt(second_new / BIAS_TWO) + ADAM_EPS)
    updated = (old_weight - LEARN_RATE * (ratio + WEIGHT_DECAY * old_weight)).astype(jnp.bfloat16)
    return (first_new, second_new, updated)


def attend(query_latent, query_rope, cache_latent, cache_rope, new_latent, new_rope, lengths):
    step_count, row_count = (query_latent.shape[0], query_latent.shape[1])
    slot_total = cache_latent.shape[1]
    query_lat = query_latent.reshape(step_count, row_count, HEADS, LAT)
    query_pos = query_rope.reshape(step_count, row_count, HEADS, ROPE)
    old_scores = (
        jnp.einsum("srhc,rlc->srhl", query_lat, cache_latent, preferred_element_type=jnp.float32)
        + jnp.einsum("srhp,rpl->srhl", query_pos, cache_rope, preferred_element_type=jnp.float32)
    ) * QK_SCALE
    new_scores = (
        jnp.einsum("srhc,trc->srht", query_lat, new_latent, preferred_element_type=jnp.float32)
        + jnp.einsum("srhp,trp->srht", query_pos, new_rope, preferred_element_type=jnp.float32)
    ) * QK_SCALE
    valid_old = jnp.arange(slot_total, dtype=jnp.int32)[None, :] < lengths[:, None]
    valid_new = jnp.arange(step_count)[None, :] <= jnp.arange(step_count)[:, None]
    old_scores = jnp.where(valid_old[None, :, None, :], old_scores, NEGATIVE)
    new_scores = jnp.where(valid_new[:, None, None, :], new_scores, NEGATIVE)
    peak_score = jnp.maximum(
        jnp.max(old_scores, -1, keepdims=True), jnp.max(new_scores, -1, keepdims=True)
    )
    old_mass = jnp.exp(old_scores - peak_score)
    new_mass = jnp.exp(new_scores - peak_score)
    total_mass = jnp.sum(old_mass, -1, keepdims=True) + jnp.sum(new_mass, -1, keepdims=True)
    old_prob = (old_mass / total_mass).astype(jnp.bfloat16)
    new_prob = (new_mass / total_mass).astype(jnp.bfloat16)
    mixture = jnp.einsum(
        "srhl,rlc->srhc", old_prob, cache_latent, preferred_element_type=jnp.float32
    ) + jnp.einsum("srht,trc->srhc", new_prob, new_latent, preferred_element_type=jnp.float32)
    summary = jnp.mean(mixture, 2)
    summary = summary * lax.rsqrt(jnp.mean(summary * summary, -1, keepdims=True) + 1e-05)
    attention_out = mixture.reshape(step_count, row_count, HEADS * LAT).astype(jnp.bfloat16)
    return (attention_out, summary.astype(jnp.bfloat16))


def local(
    weights,
    gradients,
    moment_one,
    moment_two,
    hidden_in,
    query_latent,
    query_rope,
    cache_latent,
    cache_rope,
    new_latent,
    new_rope,
    lengths,
    expert_ids,
    router,
):
    first_new, second_new, updated = adamw(weights, gradients, moment_one, moment_two)
    expert_count, slab, columns = updated.shape
    step_count, _, width = hidden_in.shape
    quarter = width // 4
    my_part = lax.all_to_all(
        jnp.swapaxes(hidden_in.reshape(step_count, 4, quarter), 0, 1),
        "tensor",
        split_axis=0,
        concat_axis=0,
        tiled=True,
    )
    slot_count = 2
    places = step_count * slot_count

    picked = (expert_ids[..., None] == jnp.arange(EXPERTS, dtype=jnp.int32)).astype(jnp.float32)
    per_expert = jnp.sum(picked, 2)
    earlier = jnp.cumsum(per_expert, 1) - per_expert
    slot_hit = (earlier[..., None] == jnp.arange(slot_count, dtype=jnp.float32)).astype(
        jnp.float32
    ) * per_expert[..., None]
    outgoing = jnp.einsum(
        "sbec,bsd->escd",
        slot_hit.astype(jnp.bfloat16),
        my_part,
        preferred_element_type=jnp.float32,
    ).astype(jnp.bfloat16)
    outgoing = outgoing.reshape(expert_count, places * quarter // 128, 128)
    slabs = jnp.swapaxes(updated.reshape(expert_count, slab, 2, 128), 1, 2)
    slabs = slabs.reshape(expert_count, 2 * slab, 128)
    payload = jnp.concatenate([slabs, outgoing], 1)
    payload, query_latent, query_rope, new_latent, new_rope = lax.optimization_barrier(
        (payload, query_latent, query_rope, new_latent, new_rope)
    )
    attention_out, summary = attend(
        query_latent, query_rope, cache_latent, cache_rope, new_latent, new_rope, lengths
    )
    arrived = lax.all_to_all(payload, "expert", split_axis=0, concat_axis=0, tiled=True)
    summary_all = lax.all_gather(summary, "tensor", axis=1, tiled=True)
    arrived, summary_all = lax.optimization_barrier((arrived, summary_all))
    held = jnp.swapaxes(arrived[:, : 2 * slab].reshape(expert_count, 2, slab, 128), 1, 2)
    held = held.reshape(expert_count * slab, columns)
    rows_in = arrived[:, 2 * slab :].reshape(expert_count * places, quarter)

    copies = jnp.broadcast_to(held[None], (lax.axis_size("group"),) + held.shape)
    whole = lax.all_to_all(copies, "group", split_axis=0, concat_axis=0, tiled=True)
    half = rows_in.shape[0] // 2
    spread = [lax.all_gather(rows_in[i * half : (i + 1) * half], "tensor") for i in range(2)]
    rows_whole = jnp.concatenate([jnp.swapaxes(x, 0, 1).reshape(half, width) for x in spread], 0)

    logits = jnp.einsum("sbc,ce->sbe", summary_all, router, preferred_element_type=jnp.float32)
    gate_prob = jax.nn.sigmoid(logits)
    chosen = jnp.sum(picked * gate_prob[:, :, None, :], -1)
    route_weight = (ROUTE_SCALE * chosen / jnp.sum(chosen, -1, keepdims=True)).astype(jnp.bfloat16)
    expert_weight = jnp.sum(picked * route_weight.astype(jnp.float32)[..., None], 2)
    combine = (slot_hit * expert_weight[..., None]).astype(jnp.bfloat16)

    whole = whole.reshape(width, columns)
    pre_act = jnp.dot(rows_whole, whole, preferred_element_type=jnp.float32)
    active = jax.nn.silu(pre_act).astype(jnp.bfloat16)
    active = active.reshape(expert_count, places, columns)
    returned = lax.all_to_all(active, "expert", split_axis=0, concat_axis=0, tiled=True)
    returned = returned.reshape(EXPERTS, step_count, slot_count, columns)
    expert_out = jnp.einsum(
        "sbec,escf->sbf", combine, returned, preferred_element_type=jnp.float32
    ).astype(jnp.bfloat16)
    return (first_new, second_new, attention_out, expert_out)


def solution(mesh):
    return jax.shard_map(
        local,
        mesh=mesh,
        in_specs=(
            P(None, ("group", "expert"), "tensor"),
            P(None, ("group", "expert"), "tensor"),
            P(None, ("group", "expert"), "tensor"),
            P(None, ("group", "expert"), "tensor"),
            P(None, ("group", "expert", "tensor"), None),
            P(None, ("group", "expert", "tensor"), None),
            P(None, ("group", "expert", "tensor"), None),
            P(("group", "expert", "tensor"), None, None),
            P(("group", "expert", "tensor"), None, None),
            P(None, ("group", "expert", "tensor"), None),
            P(None, ("group", "expert", "tensor"), None),
            P(("group", "expert", "tensor")),
            P(None, ("group", "expert"), None),
            P(),
        ),
        out_specs=(
            P(None, ("group", "expert"), "tensor"),
            P(None, ("group", "expert"), "tensor"),
            P(None, ("group", "expert", "tensor"), None),
            P(None, ("group", "expert"), "tensor"),
        ),
        check_vma=False,
    )
```

```python
import jax
import jax.numpy as jnp
from jax import lax
from jax.experimental import pallas as pl
from jax.experimental.pallas import tpu as pltpu
from jax.sharding import PartitionSpec as P

EXPERTS = 32
HEADS = 32
LAT = 512
ROPE = 64


BETA_ONE = 0.9
BETA_TWO = 0.95
LEARN_RATE = 0.005
WEIGHT_DECAY = 0.1
ADAM_EPS = 1e-08
BIAS_ONE = 1.0 - 0.9**10
BIAS_TWO = 1.0 - 0.95**10
QK_SCALE = 192.0 ** (-0.5)
ROUTE_SCALE = 2.827
NEGATIVE = -1e30


def adamw(weights, gradients, moment_one, moment_two):
    grad_wide = gradients.astype(jnp.float32)
    first_new = BETA_ONE * moment_one + (1.0 - BETA_ONE) * grad_wide
    second_new = BETA_TWO * moment_two + (1.0 - BETA_TWO) * grad_wide * grad_wide
    old_weight = weights.astype(jnp.float32)
    ratio = first_new / BIAS_ONE / (jnp.sqrt(second_new / BIAS_TWO) + ADAM_EPS)
    updated = (old_weight - LEARN_RATE * (ratio + WEIGHT_DECAY * old_weight)).astype(jnp.bfloat16)
    return (first_new, second_new, updated)


def attend(query_latent, query_rope, cache_latent, cache_rope, new_latent, new_rope, lengths):
    step_count, row_count = (query_latent.shape[0], query_latent.shape[1])
    slot_total = cache_latent.shape[1]
    query_lat = query_latent.reshape(step_count, row_count, HEADS, LAT)
    query_pos = query_rope.reshape(step_count, row_count, HEADS, ROPE)
    old_scores = (
        jnp.einsum("srhc,rlc->srhl", query_lat, cache_latent, preferred_element_type=jnp.float32)
        + jnp.einsum("srhp,rpl->srhl", query_pos, cache_rope, preferred_element_type=jnp.float32)
    ) * QK_SCALE
    new_scores = (
        jnp.einsum("srhc,trc->srht", query_lat, new_latent, preferred_element_type=jnp.float32)
        + jnp.einsum("srhp,trp->srht", query_pos, new_rope, preferred_element_type=jnp.float32)
    ) * QK_SCALE
    valid_old = jnp.arange(slot_total, dtype=jnp.int32)[None, :] < lengths[:, None]
    valid_new = jnp.arange(step_count)[None, :] <= jnp.arange(step_count)[:, None]
    old_scores = jnp.where(valid_old[None, :, None, :], old_scores, NEGATIVE)
    new_scores = jnp.where(valid_new[:, None, None, :], new_scores, NEGATIVE)
    peak_score = jnp.maximum(
        jnp.max(old_scores, -1, keepdims=True), jnp.max(new_scores, -1, keepdims=True)
    )
    old_mass = jnp.exp(old_scores - peak_score)
    new_mass = jnp.exp(new_scores - peak_score)
    total_mass = jnp.sum(old_mass, -1, keepdims=True) + jnp.sum(new_mass, -1, keepdims=True)
    old_prob = (old_mass / total_mass).astype(jnp.bfloat16)
    new_prob = (new_mass / total_mass).astype(jnp.bfloat16)
    mixture = jnp.einsum(
        "srhl,rlc->srhc", old_prob, cache_latent, preferred_element_type=jnp.float32
    ) + jnp.einsum("srht,trc->srhc", new_prob, new_latent, preferred_element_type=jnp.float32)
    summary = jnp.mean(mixture, 2)
    summary = summary * lax.rsqrt(jnp.mean(summary * summary, -1, keepdims=True) + 1e-05)
    attention_out = mixture.reshape(step_count, row_count, HEADS * LAT).astype(jnp.bfloat16)
    return (attention_out, summary.astype(jnp.bfloat16))


def flip(value, axis, distance):
    size = lax.axis_size(axis)
    return lax.ppermute(value, axis, [(i, i ^ distance) for i in range(size)])


def expert_kernel(turn_ref, own, core, far, diag, whole, out, total):
    step = pl.program_id(0)
    for index, part in enumerate((own, core, far, diag)):

        @pl.when(step == index)
        def _(index=index, part=part):
            product = jnp.dot(part[...], whole[0], preferred_element_type=jnp.float32)
            total[...] = product if index == 0 else total[...] + product

    @pl.when(step == 3)
    def _():
        value = total[...]
        out[...] = (value / (1.0 + jnp.exp(-value))).astype(out.dtype)


def expert_rows(parts, whole):
    rows, quarter = parts[0].shape
    columns = whole.shape[2]
    return pl.pallas_call(
        expert_kernel,
        out_shape=jax.ShapeDtypeStruct((rows, columns), jnp.bfloat16),
        grid_spec=pltpu.PrefetchScalarGridSpec(
            num_scalar_prefetch=1,
            grid=(4,),
            in_specs=[pl.BlockSpec((rows, quarter), lambda k, turn: (0, 0))] * 4
            + [
                pl.BlockSpec(
                    (1, quarter, columns), lambda k, turn: (jnp.bitwise_xor(k, turn[0]), 0, 0)
                )
            ],
            out_specs=pl.BlockSpec((rows, columns), lambda k, turn: (0, 0)),
            scratch_shapes=[pltpu.VMEM((rows, columns), jnp.float32)],
        ),
        compiler_params=pltpu.CompilerParams(vmem_limit_bytes=32 * 2**20),
        cost_estimate=pl.CostEstimate(
            flops=8 * rows * quarter * columns,
            bytes_accessed=8 * quarter * (rows + columns),
            transcendentals=rows * columns,
        ),
    )(lax.axis_index("tensor").reshape(1).astype(jnp.int32), *parts, whole)


def local(
    weights,
    gradients,
    moment_one,
    moment_two,
    hidden_in,
    query_latent,
    query_rope,
    cache_latent,
    cache_rope,
    new_latent,
    new_rope,
    lengths,
    expert_ids,
    router,
):
    first_new, second_new, updated = adamw(weights, gradients, moment_one, moment_two)
    expert_count, slab, columns = updated.shape
    step_count, _, width = hidden_in.shape
    quarter = width // 4
    my_part = lax.all_to_all(
        jnp.swapaxes(hidden_in.reshape(step_count, 4, quarter), 0, 1),
        "tensor",
        split_axis=0,
        concat_axis=0,
        tiled=True,
    )
    slot_count = 2
    places = step_count * slot_count

    picked = (expert_ids[..., None] == jnp.arange(EXPERTS, dtype=jnp.int32)).astype(jnp.float32)
    per_expert = jnp.sum(picked, 2)
    earlier = jnp.cumsum(per_expert, 1) - per_expert
    slot_hit = (earlier[..., None] == jnp.arange(slot_count, dtype=jnp.float32)).astype(
        jnp.float32
    ) * per_expert[..., None]
    outgoing = jnp.einsum(
        "sbec,bsd->escd",
        slot_hit.astype(jnp.bfloat16),
        my_part,
        preferred_element_type=jnp.float32,
    ).astype(jnp.bfloat16)
    outgoing = outgoing.reshape(expert_count, places * quarter // 128, 128)
    slabs = jnp.swapaxes(updated.reshape(expert_count, slab, 2, 128), 1, 2)
    slabs = slabs.reshape(expert_count, 2 * slab, 128)
    outgoing, query_latent, query_rope, new_latent, new_rope = lax.optimization_barrier(
        (outgoing, query_latent, query_rope, new_latent, new_rope)
    )
    payload = jnp.concatenate([slabs, outgoing], 1)
    attention_out, summary = attend(
        query_latent, query_rope, cache_latent, cache_rope, new_latent, new_rope, lengths
    )
    arrived = lax.all_to_all(payload, "expert", split_axis=0, concat_axis=0, tiled=True)
    summary_all = lax.all_gather(summary, "tensor", axis=1, tiled=True)
    held = jnp.swapaxes(arrived[:, : 2 * slab].reshape(expert_count, 2, slab, 128), 1, 2)
    held = held.reshape(expert_count * slab, columns)
    held, summary_all = lax.optimization_barrier((held, summary_all))
    rows_in = arrived[:, 2 * slab :].reshape(expert_count * places, quarter)

    copies = jnp.broadcast_to(held[None], (lax.axis_size("group"),) + held.shape)
    whole = lax.all_to_all(copies, "group", split_axis=0, concat_axis=0, tiled=True)
    rows_far = flip(rows_in, "tensor", 2)
    rows_core = flip(rows_in, "tensor", 1)
    rows_diag = flip(rows_far, "tensor", 1)

    logits = jnp.einsum("sbc,ce->sbe", summary_all, router, preferred_element_type=jnp.float32)
    gate_prob = jax.nn.sigmoid(logits)
    chosen = jnp.sum(picked * gate_prob[:, :, None, :], -1)
    route_weight = (ROUTE_SCALE * chosen / jnp.sum(chosen, -1, keepdims=True)).astype(jnp.bfloat16)
    expert_weight = jnp.sum(picked * route_weight.astype(jnp.float32)[..., None], 2)
    combine = (slot_hit * expert_weight[..., None]).astype(jnp.bfloat16)

    active = expert_rows((rows_in, rows_core, rows_far, rows_diag), whole)
    active = active.reshape(expert_count, places, columns)
    returned = lax.all_to_all(active, "expert", split_axis=0, concat_axis=0, tiled=True)
    returned = returned.reshape(EXPERTS, step_count, slot_count, columns)
    expert_out = jnp.einsum(
        "sbec,escf->sbf", combine, returned, preferred_element_type=jnp.float32
    ).astype(jnp.bfloat16)
    return (first_new, second_new, attention_out, expert_out)


def solution(mesh):
    return jax.shard_map(
        local,
        mesh=mesh,
        in_specs=(
            P(None, ("group", "expert"), "tensor"),
            P(None, ("group", "expert"), "tensor"),
            P(None, ("group", "expert"), "tensor"),
            P(None, ("group", "expert"), "tensor"),
            P(None, ("group", "expert", "tensor"), None),
            P(None, ("group", "expert", "tensor"), None),
            P(None, ("group", "expert", "tensor"), None),
            P(("group", "expert", "tensor"), None, None),
            P(("group", "expert", "tensor"), None, None),
            P(None, ("group", "expert", "tensor"), None),
            P(None, ("group", "expert", "tensor"), None),
            P(("group", "expert", "tensor")),
            P(None, ("group", "expert"), None),
            P(),
        ),
        out_specs=(
            P(None, ("group", "expert"), "tensor"),
            P(None, ("group", "expert"), "tensor"),
            P(None, ("group", "expert", "tensor"), None),
            P(None, ("group", "expert"), "tensor"),
        ),
        check_vma=False,
    )
```

```python
import jax
import jax.numpy as jnp
from jax import lax
from jax.experimental import pallas as pl
from jax.experimental.pallas import tpu as pltpu
from jax.sharding import PartitionSpec as P

EXPERTS = 32
HEADS = 32
LAT = 512
ROPE = 64


BETA_ONE = 0.9
BETA_TWO = 0.95
LEARN_RATE = 0.005
WEIGHT_DECAY = 0.1
ADAM_EPS = 1e-08
BIAS_ONE = 1.0 - 0.9**10
BIAS_TWO = 1.0 - 0.95**10
QK_SCALE = 192.0 ** (-0.5)
ROUTE_SCALE = 2.827
NEGATIVE = -1e30


def adamw(weights, gradients, moment_one, moment_two):
    grad_wide = gradients.astype(jnp.float32)
    first_new = BETA_ONE * moment_one + (1.0 - BETA_ONE) * grad_wide
    second_new = BETA_TWO * moment_two + (1.0 - BETA_TWO) * grad_wide * grad_wide
    old_weight = weights.astype(jnp.float32)
    ratio = first_new / BIAS_ONE / (jnp.sqrt(second_new / BIAS_TWO) + ADAM_EPS)
    updated = (old_weight - LEARN_RATE * (ratio + WEIGHT_DECAY * old_weight)).astype(jnp.bfloat16)
    return (first_new, second_new, updated)


def adamw_kernel(weights, gradients, moment_one, moment_two, first_new, second_new, updated):
    first_new[...], second_new[...], updated[...] = adamw(
        weights[...], gradients[...], moment_one[...], moment_two[...]
    )


def adamw_rows(*operands):
    operands = [jnp.swapaxes(x, 0, 1) for x in operands]
    slab, expert_count, columns = operands[0].shape
    depth = slab // 4
    block = pl.BlockSpec((depth, expert_count, columns), lambda i: (i, 0, 0))
    results = pl.pallas_call(
        adamw_kernel,
        out_shape=[
            jax.ShapeDtypeStruct(operands[0].shape, kind)
            for kind in (jnp.float32, jnp.float32, jnp.bfloat16)
        ],
        grid=(slab // depth,),
        in_specs=[block] * 4,
        out_specs=[block] * 3,
        compiler_params=pltpu.CompilerParams(vmem_limit_bytes=16 * 2**20),
        cost_estimate=pl.CostEstimate(
            flops=20 * operands[0].size,
            bytes_accessed=22 * operands[0].size,
            transcendentals=2 * operands[0].size,
        ),
    )(*operands)
    return [jnp.swapaxes(x, 0, 1) for x in results]


def attend(query_latent, query_rope, cache_latent, cache_rope, new_latent, new_rope, lengths):
    step_count, row_count = (query_latent.shape[0], query_latent.shape[1])
    slot_total = cache_latent.shape[1]
    query_lat = query_latent.reshape(step_count, row_count, HEADS, LAT)
    query_pos = query_rope.reshape(step_count, row_count, HEADS, ROPE)
    old_scores = (
        jnp.einsum("srhc,rlc->srhl", query_lat, cache_latent, preferred_element_type=jnp.float32)
        + jnp.einsum("srhp,rpl->srhl", query_pos, cache_rope, preferred_element_type=jnp.float32)
    ) * QK_SCALE
    new_scores = (
        jnp.einsum("srhc,trc->srht", query_lat, new_latent, preferred_element_type=jnp.float32)
        + jnp.einsum("srhp,trp->srht", query_pos, new_rope, preferred_element_type=jnp.float32)
    ) * QK_SCALE
    valid_old = jnp.arange(slot_total, dtype=jnp.int32)[None, :] < lengths[:, None]
    valid_new = jnp.arange(step_count)[None, :] <= jnp.arange(step_count)[:, None]
    old_scores = jnp.where(valid_old[None, :, None, :], old_scores, NEGATIVE)
    new_scores = jnp.where(valid_new[:, None, None, :], new_scores, NEGATIVE)
    peak_score = jnp.maximum(
        jnp.max(old_scores, -1, keepdims=True), jnp.max(new_scores, -1, keepdims=True)
    )
    old_mass = jnp.exp(old_scores - peak_score)
    new_mass = jnp.exp(new_scores - peak_score)
    total_mass = jnp.sum(old_mass, -1, keepdims=True) + jnp.sum(new_mass, -1, keepdims=True)
    old_prob = (old_mass / total_mass).astype(jnp.bfloat16)
    new_prob = (new_mass / total_mass).astype(jnp.bfloat16)
    mixture = jnp.einsum(
        "srhl,rlc->srhc", old_prob, cache_latent, preferred_element_type=jnp.float32
    ) + jnp.einsum("srht,trc->srhc", new_prob, new_latent, preferred_element_type=jnp.float32)
    summary = jnp.mean(mixture, 2)
    summary = summary * lax.rsqrt(jnp.mean(summary * summary, -1, keepdims=True) + 1e-05)
    attention_out = mixture.reshape(step_count, row_count, HEADS * LAT).astype(jnp.bfloat16)
    return (attention_out, summary.astype(jnp.bfloat16))


def flip(value, axis, distance):
    size = lax.axis_size(axis)
    return lax.ppermute(value, axis, [(i, i ^ distance) for i in range(size)])


def expert_kernel(turn, own, core, far, diag, whole, out):
    total = jnp.dot(own[...], whole[turn[0]], preferred_element_type=jnp.float32)
    for index, part in ((1, core), (2, far), (3, diag)):
        total = total + jnp.dot(
            part[...],
            whole[jnp.bitwise_xor(turn[0], index)],
            preferred_element_type=jnp.float32,
        )
    out[...] = (total / (1.0 + jnp.exp(-total))).astype(out.dtype)


def expert_rows(parts, whole):
    rows, quarter = parts[0].shape
    columns = whole.shape[2]
    return pl.pallas_call(
        expert_kernel,
        out_shape=jax.ShapeDtypeStruct((rows, columns), jnp.bfloat16),
        in_specs=[pl.BlockSpec(memory_space=pltpu.SMEM)]
        + [pl.BlockSpec(memory_space=pltpu.VMEM)] * 5,
        out_specs=pl.BlockSpec(memory_space=pltpu.VMEM),
        compiler_params=pltpu.CompilerParams(vmem_limit_bytes=16 * 2**20),
        cost_estimate=pl.CostEstimate(
            flops=8 * rows * quarter * columns,
            bytes_accessed=8 * quarter * (rows + columns),
            transcendentals=rows * columns,
        ),
    )(lax.axis_index("tensor").reshape(1).astype(jnp.int32), *parts, whole)


def local(
    weights,
    gradients,
    moment_one,
    moment_two,
    hidden_in,
    query_latent,
    query_rope,
    cache_latent,
    cache_rope,
    new_latent,
    new_rope,
    lengths,
    expert_ids,
    router,
):
    first_new, second_new, updated = adamw_rows(weights, gradients, moment_one, moment_two)
    expert_count, slab, columns = updated.shape
    step_count, _, width = hidden_in.shape
    quarter = width // 4
    my_part = lax.all_to_all(
        jnp.swapaxes(hidden_in.reshape(step_count, 4, quarter), 0, 1),
        "tensor",
        split_axis=0,
        concat_axis=0,
        tiled=True,
    )
    slot_count = 2
    places = step_count * slot_count

    picked = (expert_ids[..., None] == jnp.arange(EXPERTS, dtype=jnp.int32)).astype(jnp.float32)
    per_expert = jnp.sum(picked, 2)
    earlier = jnp.cumsum(per_expert, 1) - per_expert
    slot_hit = (earlier[..., None] == jnp.arange(slot_count, dtype=jnp.float32)).astype(
        jnp.float32
    ) * per_expert[..., None]
    same_step = jnp.eye(step_count, dtype=jnp.float32)
    placed = jnp.transpose(slot_hit, (1, 0, 2, 3))[:, :, :, None] * same_step[:, None, :, None]
    placed = placed.reshape(4 * step_count, expert_count * places)
    outgoing = lax.dot_general(
        placed.astype(jnp.bfloat16),
        my_part.reshape(4 * step_count, quarter),
        (((0,), (0,)), ((), ())),
        preferred_element_type=jnp.float32,
    ).astype(jnp.bfloat16)
    lanes = quarter // 128
    outgoing = jnp.swapaxes(outgoing.reshape(expert_count, places, lanes, 128), 1, 2)
    outgoing = outgoing.reshape(expert_count, places * lanes, 128)
    slabs = jnp.swapaxes(updated.reshape(expert_count, slab, 2, 128), 1, 2)
    slabs = slabs.reshape(expert_count, 2 * slab, 128)
    outgoing, query_latent, query_rope, new_latent, new_rope = lax.optimization_barrier(
        (outgoing, query_latent, query_rope, new_latent, new_rope)
    )
    payload = jnp.concatenate([slabs, outgoing], 1)
    attention_out, summary = attend(
        query_latent, query_rope, cache_latent, cache_rope, new_latent, new_rope, lengths
    )
    arrived = lax.all_to_all(payload, "expert", split_axis=0, concat_axis=0, tiled=True)
    summary_all = lax.all_gather(summary, "tensor", axis=1, tiled=True)
    held = jnp.swapaxes(arrived[:, : 2 * slab].reshape(expert_count, 2, slab, 128), 1, 2)
    held = held.reshape(expert_count * slab, columns)
    held, summary_all = lax.optimization_barrier((held, summary_all))
    rows_in = arrived[:, 2 * slab :].reshape(expert_count, lanes, places, 128)
    rows_in = jnp.swapaxes(rows_in, 1, 2).reshape(expert_count * places, quarter)

    copies = jnp.broadcast_to(held[None], (lax.axis_size("group"),) + held.shape)
    whole = lax.all_to_all(copies, "group", split_axis=0, concat_axis=0, tiled=True)
    rows_far = flip(rows_in, "tensor", 2)
    rows_core = flip(rows_in, "tensor", 1)
    rows_diag = flip(rows_far, "tensor", 1)

    logits = jnp.einsum("sbc,ce->sbe", summary_all, router, preferred_element_type=jnp.float32)
    gate_prob = jax.nn.sigmoid(logits)
    chosen = jnp.sum(picked * gate_prob[:, :, None, :], -1)
    route_weight = (ROUTE_SCALE * chosen / jnp.sum(chosen, -1, keepdims=True)).astype(jnp.bfloat16)
    expert_weight = jnp.sum(picked * route_weight.astype(jnp.float32)[..., None], 2)
    share = jnp.transpose(expert_weight, (1, 0, 2))[..., None, None]
    combine = placed.reshape(4, step_count, expert_count, step_count, slot_count) * share
    combine = combine.reshape(4 * step_count, expert_count * places).astype(jnp.bfloat16)

    active = expert_rows((rows_in, rows_core, rows_far, rows_diag), whole)
    active = active.reshape(expert_count, places, columns)
    returned = lax.all_to_all(active, "expert", split_axis=0, concat_axis=0, tiled=True)
    expert_out = jnp.dot(
        combine,
        returned.reshape(expert_count * places, columns),
        preferred_element_type=jnp.float32,
    ).astype(jnp.bfloat16)
    expert_out = jnp.swapaxes(expert_out.reshape(4, step_count, columns), 0, 1)
    return (first_new, second_new, attention_out, expert_out)


def solution(mesh):
    return jax.shard_map(
        local,
        mesh=mesh,
        in_specs=(
            P(None, ("group", "expert"), "tensor"),
            P(None, ("group", "expert"), "tensor"),
            P(None, ("group", "expert"), "tensor"),
            P(None, ("group", "expert"), "tensor"),
            P(None, ("group", "expert", "tensor"), None),
            P(None, ("group", "expert", "tensor"), None),
            P(None, ("group", "expert", "tensor"), None),
            P(("group", "expert", "tensor"), None, None),
            P(("group", "expert", "tensor"), None, None),
            P(None, ("group", "expert", "tensor"), None),
            P(None, ("group", "expert", "tensor"), None),
            P(("group", "expert", "tensor")),
            P(None, ("group", "expert"), None),
            P(),
        ),
        out_specs=(
            P(None, ("group", "expert"), "tensor"),
            P(None, ("group", "expert"), "tensor"),
            P(None, ("group", "expert", "tensor"), None),
            P(None, ("group", "expert"), "tensor"),
        ),
        check_vma=False,
    )
```

```python
import jax
import jax.numpy as jnp
from jax import lax
from jax.experimental import pallas as pl
from jax.experimental.pallas import tpu as pltpu
from jax.sharding import PartitionSpec as P

EXPERTS = 32
HEADS = 32
LAT = 512
ROPE = 64


BETA_ONE = 0.9
BETA_TWO = 0.95
LEARN_RATE = 0.005
WEIGHT_DECAY = 0.1
ADAM_EPS = 1e-08
BIAS_ONE = 1.0 - 0.9**10
BIAS_TWO = 1.0 - 0.95**10
QK_SCALE = 192.0 ** (-0.5)
ROUTE_SCALE = 2.827
NEGATIVE = -1e30


def adamw(weights, gradients, moment_one, moment_two):
    grad_wide = gradients.astype(jnp.float32)
    first_new = BETA_ONE * moment_one + (1.0 - BETA_ONE) * grad_wide
    second_new = BETA_TWO * moment_two + (1.0 - BETA_TWO) * grad_wide * grad_wide
    old_weight = weights.astype(jnp.float32)
    ratio = first_new / BIAS_ONE / (jnp.sqrt(second_new / BIAS_TWO) + ADAM_EPS)
    updated = (old_weight - LEARN_RATE * (ratio + WEIGHT_DECAY * old_weight)).astype(jnp.bfloat16)
    return (first_new, second_new, updated)


def attend(query_latent, query_rope, cache_latent, cache_rope, new_latent, new_rope, lengths):
    step_count, row_count = (query_latent.shape[0], query_latent.shape[1])
    slot_total = cache_latent.shape[1]
    query_lat = query_latent.reshape(step_count, row_count, HEADS, LAT)
    query_pos = query_rope.reshape(step_count, row_count, HEADS, ROPE)
    old_scores = (
        jnp.einsum("srhc,rlc->srhl", query_lat, cache_latent, preferred_element_type=jnp.float32)
        + jnp.einsum("srhp,rpl->srhl", query_pos, cache_rope, preferred_element_type=jnp.float32)
    ) * QK_SCALE
    new_scores = (
        jnp.einsum("srhc,trc->srht", query_lat, new_latent, preferred_element_type=jnp.float32)
        + jnp.einsum("srhp,trp->srht", query_pos, new_rope, preferred_element_type=jnp.float32)
    ) * QK_SCALE
    valid_old = jnp.arange(slot_total, dtype=jnp.int32)[None, :] < lengths[:, None]
    valid_new = jnp.arange(step_count)[None, :] <= jnp.arange(step_count)[:, None]
    old_scores = jnp.where(valid_old[None, :, None, :], old_scores, NEGATIVE)
    new_scores = jnp.where(valid_new[:, None, None, :], new_scores, NEGATIVE)
    peak_score = jnp.maximum(
        jnp.max(old_scores, -1, keepdims=True), jnp.max(new_scores, -1, keepdims=True)
    )
    old_mass = jnp.exp(old_scores - peak_score)
    new_mass = jnp.exp(new_scores - peak_score)
    total_mass = jnp.sum(old_mass, -1, keepdims=True) + jnp.sum(new_mass, -1, keepdims=True)
    old_prob = (old_mass / total_mass).astype(jnp.bfloat16)
    new_prob = (new_mass / total_mass).astype(jnp.bfloat16)
    mixture = jnp.einsum(
        "srhl,rlc->srhc", old_prob, cache_latent, preferred_element_type=jnp.float32
    ) + jnp.einsum("srht,trc->srhc", new_prob, new_latent, preferred_element_type=jnp.float32)
    summary = jnp.mean(mixture, 2)
    summary = summary * lax.rsqrt(jnp.mean(summary * summary, -1, keepdims=True) + 1e-05)
    attention_out = mixture.reshape(step_count, row_count, HEADS * LAT).astype(jnp.bfloat16)
    return (attention_out, summary.astype(jnp.bfloat16))


def flip(value, axis, distance):
    size = lax.axis_size(axis)
    return lax.ppermute(value, axis, [(i, i ^ distance) for i in range(size)])


def expert_kernel(turn, own, core, far, diag, whole, out, last, arrival):
    fetch = pltpu.make_async_copy(diag, last, arrival)
    fetch.start()
    total = jnp.dot(own[...], whole[turn[0]], preferred_element_type=jnp.float32)
    for index, part in ((1, core), (2, far), (3, last)):
        if index == 3:
            fetch.wait()
        total = total + jnp.dot(
            part[...],
            whole[jnp.bitwise_xor(turn[0], index)],
            preferred_element_type=jnp.float32,
        )
    out[...] = (total / (1.0 + jnp.exp(-total))).astype(out.dtype)


def expert_rows(parts, whole):
    rows, quarter = parts[0].shape
    columns = whole.shape[2]
    return pl.pallas_call(
        expert_kernel,
        out_shape=jax.ShapeDtypeStruct((rows, columns), jnp.bfloat16),
        in_specs=[pl.BlockSpec(memory_space=pltpu.SMEM)]
        + [pl.BlockSpec(memory_space=pltpu.VMEM)] * 3
        + [pl.BlockSpec(memory_space=pl.ANY), pl.BlockSpec(memory_space=pltpu.VMEM)],
        out_specs=pl.BlockSpec(memory_space=pltpu.VMEM),
        scratch_shapes=[pltpu.VMEM((rows, quarter), jnp.bfloat16), pltpu.SemaphoreType.DMA],
        compiler_params=pltpu.CompilerParams(vmem_limit_bytes=16 * 2**20),
        cost_estimate=pl.CostEstimate(
            flops=8 * rows * quarter * columns,
            bytes_accessed=8 * quarter * (rows + columns),
            transcendentals=rows * columns,
        ),
    )(lax.axis_index("tensor").reshape(1).astype(jnp.int32), *parts, whole)


def local(
    weights,
    gradients,
    moment_one,
    moment_two,
    hidden_in,
    query_latent,
    query_rope,
    cache_latent,
    cache_rope,
    new_latent,
    new_rope,
    lengths,
    expert_ids,
    router,
):
    first_new, second_new, updated = adamw(weights, gradients, moment_one, moment_two)
    expert_count, slab, columns = updated.shape
    step_count, _, width = hidden_in.shape
    quarter = width // 4
    my_part = lax.all_to_all(
        jnp.swapaxes(hidden_in.reshape(step_count, 4, quarter), 0, 1),
        "tensor",
        split_axis=0,
        concat_axis=0,
        tiled=True,
    )
    slot_count = 2
    places = step_count * slot_count

    picked = (expert_ids[..., None] == jnp.arange(EXPERTS, dtype=jnp.int32)).astype(jnp.float32)
    per_expert = jnp.sum(picked, 2)
    earlier = jnp.cumsum(per_expert, 1) - per_expert
    slot_hit = (earlier[..., None] == jnp.arange(slot_count, dtype=jnp.float32)).astype(
        jnp.float32
    ) * per_expert[..., None]
    outgoing = jnp.einsum(
        "sbec,bsd->escd",
        slot_hit.astype(jnp.bfloat16),
        my_part,
        preferred_element_type=jnp.float32,
    ).astype(jnp.bfloat16)
    outgoing = outgoing.reshape(expert_count, places * quarter // 128, 128)
    slabs = jnp.swapaxes(updated.reshape(expert_count, slab, 2, 128), 1, 2)
    slabs = slabs.reshape(expert_count, 2 * slab, 128)
    outgoing, query_latent, query_rope, new_latent, new_rope = lax.optimization_barrier(
        (outgoing, query_latent, query_rope, new_latent, new_rope)
    )
    payload = jnp.concatenate([slabs, outgoing], 1)
    attention_out, summary = attend(
        query_latent, query_rope, cache_latent, cache_rope, new_latent, new_rope, lengths
    )
    arrived = lax.all_to_all(payload, "expert", split_axis=0, concat_axis=0, tiled=True)
    summary_all = lax.all_gather(summary, "tensor", axis=1, tiled=True)
    held = jnp.swapaxes(arrived[:, : 2 * slab].reshape(expert_count, 2, slab, 128), 1, 2)
    held = held.reshape(expert_count * slab, columns)
    held, summary_all = lax.optimization_barrier((held, summary_all))
    rows_in = arrived[:, 2 * slab :].reshape(expert_count * places, quarter)

    copies = jnp.broadcast_to(held[None], (lax.axis_size("group"),) + held.shape)
    whole = lax.all_to_all(copies, "group", split_axis=0, concat_axis=0, tiled=True)
    rows_far = flip(rows_in, "tensor", 2)
    rows_core = flip(rows_in, "tensor", 1)
    rows_diag = flip(rows_far, "tensor", 1)

    logits = jnp.einsum("sbc,ce->sbe", summary_all, router, preferred_element_type=jnp.float32)
    gate_prob = jax.nn.sigmoid(logits)
    chosen = jnp.sum(picked * gate_prob[:, :, None, :], -1)
    route_weight = (ROUTE_SCALE * chosen / jnp.sum(chosen, -1, keepdims=True)).astype(jnp.bfloat16)
    expert_weight = jnp.sum(picked * route_weight.astype(jnp.float32)[..., None], 2)
    combine = (slot_hit * expert_weight[..., None]).astype(jnp.bfloat16)

    active = expert_rows((rows_in, rows_core, rows_far, rows_diag), whole)
    active = active.reshape(expert_count, places, columns)
    returned = lax.all_to_all(active, "expert", split_axis=0, concat_axis=0, tiled=True)
    returned = returned.reshape(EXPERTS, step_count, slot_count, columns)
    expert_out = jnp.einsum(
        "sbec,escf->sbf", combine, returned, preferred_element_type=jnp.float32
    ).astype(jnp.bfloat16)
    return (first_new, second_new, attention_out, expert_out)


def solution(mesh):
    return jax.shard_map(
        local,
        mesh=mesh,
        in_specs=(
            P(None, ("group", "expert"), "tensor"),
            P(None, ("group", "expert"), "tensor"),
            P(None, ("group", "expert"), "tensor"),
            P(None, ("group", "expert"), "tensor"),
            P(None, ("group", "expert", "tensor"), None),
            P(None, ("group", "expert", "tensor"), None),
            P(None, ("group", "expert", "tensor"), None),
            P(("group", "expert", "tensor"), None, None),
            P(("group", "expert", "tensor"), None, None),
            P(None, ("group", "expert", "tensor"), None),
            P(None, ("group", "expert", "tensor"), None),
            P(("group", "expert", "tensor")),
            P(None, ("group", "expert"), None),
            P(),
        ),
        out_specs=(
            P(None, ("group", "expert"), "tensor"),
            P(None, ("group", "expert"), "tensor"),
            P(None, ("group", "expert", "tensor"), None),
            P(None, ("group", "expert"), "tensor"),
        ),
        check_vma=False,
    )
```

```python
import jax
import jax.numpy as jnp
from jax import lax
from jax.experimental import pallas as pl
from jax.experimental.pallas import tpu as pltpu
from jax.sharding import PartitionSpec as P

EXPERTS = 32
HEADS = 32
LAT = 512
ROPE = 64


BETA_ONE = 0.9
BETA_TWO = 0.95
LEARN_RATE = 0.005
WEIGHT_DECAY = 0.1
ADAM_EPS = 1e-08
BIAS_ONE = 1.0 - 0.9**10
BIAS_TWO = 1.0 - 0.95**10
QK_SCALE = 192.0 ** (-0.5)
ROUTE_SCALE = 2.827
NEGATIVE = -1e30


def adamw(weights, gradients, moment_one, moment_two):
    grad_wide = gradients.astype(jnp.float32)
    first_new = BETA_ONE * moment_one + (1.0 - BETA_ONE) * grad_wide
    second_new = BETA_TWO * moment_two + (1.0 - BETA_TWO) * grad_wide * grad_wide
    old_weight = weights.astype(jnp.float32)
    ratio = first_new / BIAS_ONE / (jnp.sqrt(second_new / BIAS_TWO) + ADAM_EPS)
    updated = (old_weight - LEARN_RATE * (ratio + WEIGHT_DECAY * old_weight)).astype(jnp.bfloat16)
    return (first_new, second_new, updated)


def attend(query_latent, query_rope, cache_latent, cache_rope, new_latent, new_rope, lengths):
    step_count, row_count = (query_latent.shape[0], query_latent.shape[1])
    slot_total = cache_latent.shape[1]
    query_lat = query_latent.reshape(step_count, row_count, HEADS, LAT)
    query_pos = query_rope.reshape(step_count, row_count, HEADS, ROPE)
    old_scores = (
        jnp.einsum("srhc,rlc->srhl", query_lat, cache_latent, preferred_element_type=jnp.float32)
        + jnp.einsum("srhp,rpl->srhl", query_pos, cache_rope, preferred_element_type=jnp.float32)
    ) * QK_SCALE
    new_scores = (
        jnp.einsum("srhc,trc->srht", query_lat, new_latent, preferred_element_type=jnp.float32)
        + jnp.einsum("srhp,trp->srht", query_pos, new_rope, preferred_element_type=jnp.float32)
    ) * QK_SCALE
    valid_old = jnp.arange(slot_total, dtype=jnp.int32)[None, :] < lengths[:, None]
    valid_new = jnp.arange(step_count)[None, :] <= jnp.arange(step_count)[:, None]
    old_scores = jnp.where(valid_old[None, :, None, :], old_scores, NEGATIVE)
    new_scores = jnp.where(valid_new[:, None, None, :], new_scores, NEGATIVE)
    peak_score = jnp.maximum(
        jnp.max(old_scores, -1, keepdims=True), jnp.max(new_scores, -1, keepdims=True)
    )
    old_mass = jnp.exp(old_scores - peak_score)
    new_mass = jnp.exp(new_scores - peak_score)
    total_mass = jnp.sum(old_mass, -1, keepdims=True) + jnp.sum(new_mass, -1, keepdims=True)
    old_prob = (old_mass / total_mass).astype(jnp.bfloat16)
    new_prob = (new_mass / total_mass).astype(jnp.bfloat16)
    mixture = jnp.einsum(
        "srhl,rlc->srhc", old_prob, cache_latent, preferred_element_type=jnp.float32
    ) + jnp.einsum("srht,trc->srhc", new_prob, new_latent, preferred_element_type=jnp.float32)
    summary = jnp.mean(mixture, 2)
    summary = summary * lax.rsqrt(jnp.mean(summary * summary, -1, keepdims=True) + 1e-05)
    attention_out = mixture.reshape(step_count, row_count, HEADS * LAT).astype(jnp.bfloat16)
    return (attention_out, summary.astype(jnp.bfloat16))


def flip(value, axis, distance):
    size = lax.axis_size(axis)
    return lax.ppermute(value, axis, [(i, i ^ distance) for i in range(size)])


def expert_kernel(turn, own, core, far, diag, whole, out, last, arrival):
    fetch = pltpu.make_async_copy(diag, last, arrival)
    fetch.start()
    total = jnp.dot(own[...], whole[turn[0]], preferred_element_type=jnp.float32)
    for index, part in ((1, core), (2, far), (3, last)):
        if index == 3:
            fetch.wait()
        total = total + jnp.dot(
            part[...],
            whole[jnp.bitwise_xor(turn[0], index)],
            preferred_element_type=jnp.float32,
        )
    out[...] = (total / (1.0 + jnp.exp(-total))).astype(out.dtype)


def expert_rows(parts, whole):
    rows, quarter = parts[0].shape
    columns = whole.shape[2]
    return pl.pallas_call(
        expert_kernel,
        out_shape=jax.ShapeDtypeStruct((rows, columns), jnp.bfloat16),
        in_specs=[pl.BlockSpec(memory_space=pltpu.SMEM)]
        + [pl.BlockSpec(memory_space=pltpu.VMEM)] * 3
        + [pl.BlockSpec(memory_space=pl.ANY), pl.BlockSpec(memory_space=pltpu.VMEM)],
        out_specs=pl.BlockSpec(memory_space=pltpu.VMEM),
        scratch_shapes=[pltpu.VMEM((rows, quarter), jnp.bfloat16), pltpu.SemaphoreType.DMA],
        compiler_params=pltpu.CompilerParams(vmem_limit_bytes=16 * 2**20),
        cost_estimate=pl.CostEstimate(
            flops=8 * rows * quarter * columns,
            bytes_accessed=8 * quarter * (rows + columns),
            transcendentals=rows * columns,
        ),
    )(lax.axis_index("tensor").reshape(1).astype(jnp.int32), *parts, whole)


def local(
    weights,
    gradients,
    moment_one,
    moment_two,
    hidden_in,
    query_latent,
    query_rope,
    cache_latent,
    cache_rope,
    new_latent,
    new_rope,
    lengths,
    expert_ids,
    router,
):
    expert_count, slab, columns = weights.shape
    step_count, _, width = hidden_in.shape
    quarter = width // 4
    my_part = lax.all_to_all(
        jnp.swapaxes(hidden_in.reshape(step_count, 4, quarter), 0, 1),
        "tensor",
        split_axis=0,
        concat_axis=0,
        tiled=True,
    )
    slot_count = 2
    places = step_count * slot_count

    picked = (expert_ids[..., None] == jnp.arange(EXPERTS, dtype=jnp.int32)).astype(jnp.float32)
    per_expert = jnp.sum(picked, 2)
    earlier = jnp.cumsum(per_expert, 1) - per_expert
    slot_hit = (earlier[..., None] == jnp.arange(slot_count, dtype=jnp.float32)).astype(
        jnp.float32
    ) * per_expert[..., None]
    same_step = jnp.eye(step_count, dtype=jnp.float32)
    placed = jnp.transpose(slot_hit, (1, 0, 2, 3))[:, :, :, None] * same_step[:, None, :, None]
    placed = placed.reshape(4 * step_count, expert_count * places).astype(jnp.bfloat16)
    placed, weights = lax.optimization_barrier((placed, weights))
    updated = adamw(weights, gradients, moment_one, moment_two)[2]
    outgoing = lax.dot_general(
        placed,
        my_part.reshape(4 * step_count, quarter),
        (((0,), (0,)), ((), ())),
        preferred_element_type=jnp.float32,
    ).astype(jnp.bfloat16)
    lanes = quarter // 128
    outgoing = jnp.swapaxes(outgoing.reshape(expert_count, places, lanes, 128), 1, 2)
    outgoing = outgoing.reshape(expert_count, places * lanes, 128)
    slabs = jnp.swapaxes(updated.reshape(expert_count, slab, 2, 128), 1, 2)
    slabs = slabs.reshape(expert_count, 2 * slab, 128)
    outgoing, query_latent, query_rope, new_latent, new_rope, gradients, moment_one, moment_two = (
        lax.optimization_barrier(
            (
                outgoing,
                query_latent,
                query_rope,
                new_latent,
                new_rope,
                gradients,
                moment_one,
                moment_two,
            )
        )
    )
    payload = jnp.concatenate([slabs, outgoing], 1)
    first_new, second_new, _ = adamw(weights, gradients, moment_one, moment_two)
    attention_out, summary = attend(
        query_latent, query_rope, cache_latent, cache_rope, new_latent, new_rope, lengths
    )
    arrived = lax.all_to_all(payload, "expert", split_axis=0, concat_axis=0, tiled=True)
    summary_all = lax.all_gather(summary, "tensor", axis=1, tiled=True)
    held = jnp.swapaxes(arrived[:, : 2 * slab].reshape(expert_count, 2, slab, 128), 1, 2)
    held = held.reshape(expert_count * slab, columns)
    held, summary_all = lax.optimization_barrier((held, summary_all))
    rows_in = arrived[:, 2 * slab :].reshape(expert_count, lanes, places, 128)
    rows_in = jnp.swapaxes(rows_in, 1, 2).reshape(expert_count * places, quarter)

    copies = jnp.broadcast_to(held[None], (lax.axis_size("group"),) + held.shape)
    whole = lax.all_to_all(copies, "group", split_axis=0, concat_axis=0, tiled=True)
    rows_far = flip(rows_in, "tensor", 2)
    rows_core = flip(rows_in, "tensor", 1)
    rows_diag = flip(rows_far, "tensor", 1)

    logits = jnp.einsum("sbc,ce->sbe", summary_all, router, preferred_element_type=jnp.float32)
    gate_prob = jax.nn.sigmoid(logits)
    chosen = jnp.sum(picked * gate_prob[:, :, None, :], -1)
    route_weight = (ROUTE_SCALE * chosen / jnp.sum(chosen, -1, keepdims=True)).astype(jnp.bfloat16)
    expert_weight = jnp.sum(picked * route_weight.astype(jnp.float32)[..., None], 2)
    combine = (slot_hit * expert_weight[..., None]).astype(jnp.bfloat16)

    active = expert_rows((rows_in, rows_core, rows_far, rows_diag), whole)
    active = active.reshape(expert_count, places, columns)
    returned = lax.all_to_all(active, "expert", split_axis=0, concat_axis=0, tiled=True)
    returned = returned.reshape(EXPERTS, step_count, slot_count, columns)
    expert_out = jnp.einsum(
        "sbec,escf->sbf", combine, returned, preferred_element_type=jnp.float32
    ).astype(jnp.bfloat16)
    return (first_new, second_new, attention_out, expert_out)


def solution(mesh):
    return jax.shard_map(
        local,
        mesh=mesh,
        in_specs=(
            P(None, ("group", "expert"), "tensor"),
            P(None, ("group", "expert"), "tensor"),
            P(None, ("group", "expert"), "tensor"),
            P(None, ("group", "expert"), "tensor"),
            P(None, ("group", "expert", "tensor"), None),
            P(None, ("group", "expert", "tensor"), None),
            P(None, ("group", "expert", "tensor"), None),
            P(("group", "expert", "tensor"), None, None),
            P(("group", "expert", "tensor"), None, None),
            P(None, ("group", "expert", "tensor"), None),
            P(None, ("group", "expert", "tensor"), None),
            P(("group", "expert", "tensor")),
            P(None, ("group", "expert"), None),
            P(),
        ),
        out_specs=(
            P(None, ("group", "expert"), "tensor"),
            P(None, ("group", "expert"), "tensor"),
            P(None, ("group", "expert", "tensor"), None),
            P(None, ("group", "expert"), "tensor"),
        ),
        check_vma=False,
    )
```

```python
import jax
import jax.numpy as jnp
from jax import lax
from jax.experimental import pallas as pl
from jax.experimental.pallas import tpu as pltpu
from jax.sharding import PartitionSpec as P

EXPERTS = 32
HEADS = 32
LAT = 512
ROPE = 64


BETA_ONE = 0.9
BETA_TWO = 0.95
LEARN_RATE = 0.005
WEIGHT_DECAY = 0.1
ADAM_EPS = 1e-08
BIAS_ONE = 1.0 - 0.9**10
BIAS_TWO = 1.0 - 0.95**10
QK_SCALE = 192.0 ** (-0.5)
ROUTE_SCALE = 2.827
NEGATIVE = -1e30


def adamw(weights, gradients, moment_one, moment_two):
    grad_wide = gradients.astype(jnp.float32)
    first_new = BETA_ONE * moment_one + (1.0 - BETA_ONE) * grad_wide
    second_new = BETA_TWO * moment_two + (1.0 - BETA_TWO) * grad_wide * grad_wide
    old_weight = weights.astype(jnp.float32)
    ratio = first_new / BIAS_ONE / (jnp.sqrt(second_new / BIAS_TWO) + ADAM_EPS)
    updated = (old_weight - LEARN_RATE * (ratio + WEIGHT_DECAY * old_weight)).astype(jnp.bfloat16)
    return (first_new, second_new, updated)


def attend(query_latent, query_rope, cache_latent, cache_rope, new_latent, new_rope, lengths):
    step_count, row_count = (query_latent.shape[0], query_latent.shape[1])
    slot_total = cache_latent.shape[1]
    query_lat = query_latent.reshape(step_count, row_count, HEADS, LAT)
    query_pos = query_rope.reshape(step_count, row_count, HEADS, ROPE)
    old_scores = (
        jnp.einsum("srhc,rlc->srhl", query_lat, cache_latent, preferred_element_type=jnp.float32)
        + jnp.einsum("srhp,rpl->srhl", query_pos, cache_rope, preferred_element_type=jnp.float32)
    ) * QK_SCALE
    new_scores = (
        jnp.einsum("srhc,trc->srht", query_lat, new_latent, preferred_element_type=jnp.float32)
        + jnp.einsum("srhp,trp->srht", query_pos, new_rope, preferred_element_type=jnp.float32)
    ) * QK_SCALE
    valid_old = jnp.arange(slot_total, dtype=jnp.int32)[None, :] < lengths[:, None]
    valid_new = jnp.arange(step_count)[None, :] <= jnp.arange(step_count)[:, None]
    old_scores = jnp.where(valid_old[None, :, None, :], old_scores, NEGATIVE)
    new_scores = jnp.where(valid_new[:, None, None, :], new_scores, NEGATIVE)
    peak_score = jnp.maximum(
        jnp.max(old_scores, -1, keepdims=True), jnp.max(new_scores, -1, keepdims=True)
    )
    old_mass = jnp.exp(old_scores - peak_score)
    new_mass = jnp.exp(new_scores - peak_score)
    total_mass = jnp.sum(old_mass, -1, keepdims=True) + jnp.sum(new_mass, -1, keepdims=True)
    old_prob = (old_mass / total_mass).astype(jnp.bfloat16)
    new_prob = (new_mass / total_mass).astype(jnp.bfloat16)
    mixture = jnp.einsum(
        "srhl,rlc->srhc", old_prob, cache_latent, preferred_element_type=jnp.float32
    ) + jnp.einsum("srht,trc->srhc", new_prob, new_latent, preferred_element_type=jnp.float32)
    summary = jnp.mean(mixture, 2)
    summary = summary * lax.rsqrt(jnp.mean(summary * summary, -1, keepdims=True) + 1e-05)
    attention_out = mixture.reshape(step_count, row_count, HEADS * LAT).astype(jnp.bfloat16)
    return (attention_out, summary.astype(jnp.bfloat16))


def flip(value, axis, distance):
    size = lax.axis_size(axis)
    return lax.ppermute(value, axis, [(i, i ^ distance) for i in range(size)])


def expert_kernel(turn, own, core, far, diag, whole, out, last, arrival):
    fetch = pltpu.make_async_copy(diag, last, arrival)
    fetch.start()
    total = jnp.dot(own[...], whole[turn[0]], preferred_element_type=jnp.float32)
    for index, part in ((1, core), (2, far), (3, last)):
        if index == 3:
            fetch.wait()
        total = total + jnp.dot(
            part[...],
            whole[jnp.bitwise_xor(turn[0], index)],
            preferred_element_type=jnp.float32,
        )
    out[...] = (total / (1.0 + jnp.exp(-total))).astype(out.dtype)


def expert_rows(parts, whole):
    rows, quarter = parts[0].shape
    columns = whole.shape[2]
    return pl.pallas_call(
        expert_kernel,
        out_shape=jax.ShapeDtypeStruct((rows, columns), jnp.bfloat16),
        in_specs=[pl.BlockSpec(memory_space=pltpu.SMEM)]
        + [pl.BlockSpec(memory_space=pltpu.VMEM)] * 3
        + [pl.BlockSpec(memory_space=pl.ANY), pl.BlockSpec(memory_space=pltpu.VMEM)],
        out_specs=pl.BlockSpec(memory_space=pltpu.VMEM),
        scratch_shapes=[pltpu.VMEM((rows, quarter), jnp.bfloat16), pltpu.SemaphoreType.DMA],
        compiler_params=pltpu.CompilerParams(vmem_limit_bytes=16 * 2**20),
        cost_estimate=pl.CostEstimate(
            flops=8 * rows * quarter * columns,
            bytes_accessed=8 * quarter * (rows + columns),
            transcendentals=rows * columns,
        ),
    )(lax.axis_index("tensor").reshape(1).astype(jnp.int32), *parts, whole)


def local(
    weights,
    gradients,
    moment_one,
    moment_two,
    hidden_in,
    query_latent,
    query_rope,
    cache_latent,
    cache_rope,
    new_latent,
    new_rope,
    lengths,
    expert_ids,
    router,
):
    expert_count, slab, columns = weights.shape
    step_count, _, width = hidden_in.shape
    quarter = width // 4
    my_part = lax.all_to_all(
        jnp.swapaxes(hidden_in.reshape(step_count, 4, quarter), 0, 1),
        "tensor",
        split_axis=0,
        concat_axis=0,
        tiled=True,
    )
    slot_count = 2
    places = step_count * slot_count

    picked = (expert_ids[..., None] == jnp.arange(EXPERTS, dtype=jnp.int32)).astype(jnp.float32)
    per_expert = jnp.sum(picked, 2)
    earlier = jnp.cumsum(per_expert, 1) - per_expert
    slot_hit = (earlier[..., None] == jnp.arange(slot_count, dtype=jnp.float32)).astype(
        jnp.float32
    ) * per_expert[..., None]
    same_step = jnp.eye(step_count, dtype=jnp.float32)
    placed = jnp.transpose(slot_hit, (1, 0, 2, 3))[:, :, :, None] * same_step[:, None, :, None]
    placed = placed.reshape(4 * step_count, expert_count * places).astype(jnp.bfloat16)
    placed, weights = lax.optimization_barrier((placed, weights))
    updated = adamw(weights, gradients, moment_one, moment_two)[2]
    outgoing = lax.dot_general(
        placed,
        my_part.reshape(4 * step_count, quarter),
        (((0,), (0,)), ((), ())),
        preferred_element_type=jnp.float32,
    ).astype(jnp.bfloat16)
    lanes = quarter // 128
    outgoing = jnp.swapaxes(outgoing.reshape(expert_count, places, lanes, 128), 1, 2)
    outgoing = outgoing.reshape(expert_count, places * lanes, 128)
    slabs = jnp.swapaxes(updated.reshape(expert_count, slab, 2, 128), 1, 2)
    slabs = slabs.reshape(expert_count, 2 * slab, 128)
    outgoing, query_latent, query_rope, new_latent, new_rope, gradients, moment_one, moment_two = (
        lax.optimization_barrier(
            (
                outgoing,
                query_latent,
                query_rope,
                new_latent,
                new_rope,
                gradients,
                moment_one,
                moment_two,
            )
        )
    )
    payload = jnp.concatenate([slabs, outgoing], 1)
    first_new, second_new, _ = adamw(weights, gradients, moment_one, moment_two)
    attention_out, summary = attend(
        query_latent, query_rope, cache_latent, cache_rope, new_latent, new_rope, lengths
    )
    arrived = lax.all_to_all(payload, "expert", split_axis=0, concat_axis=0, tiled=True)
    summary_all = lax.all_gather(summary, "tensor", axis=1, tiled=True)
    logits = jnp.einsum("sbc,ce->sbe", summary_all, router, preferred_element_type=jnp.float32)
    gate_prob = jax.nn.sigmoid(logits)
    chosen = jnp.sum(picked * gate_prob[:, :, None, :], -1)
    route_weight = (ROUTE_SCALE * chosen / jnp.sum(chosen, -1, keepdims=True)).astype(jnp.bfloat16)
    expert_weight = jnp.sum(picked * route_weight.astype(jnp.float32)[..., None], 2)
    combine = (slot_hit * expert_weight[..., None]).astype(jnp.bfloat16)

    held = jnp.swapaxes(arrived[:, : 2 * slab].reshape(expert_count, 2, slab, 128), 1, 2)
    held = held.reshape(expert_count * slab, columns)
    held, combine, first_new, second_new, attention_out = lax.optimization_barrier(
        (held, combine, first_new, second_new, attention_out)
    )
    rows_in = arrived[:, 2 * slab :].reshape(expert_count, lanes, places, 128)
    rows_in = jnp.swapaxes(rows_in, 1, 2).reshape(expert_count * places, quarter)

    copies = jnp.broadcast_to(held[None], (lax.axis_size("group"),) + held.shape)
    whole = lax.all_to_all(copies, "group", split_axis=0, concat_axis=0, tiled=True)
    rows_far = flip(rows_in, "tensor", 2)
    rows_core = flip(rows_in, "tensor", 1)
    rows_diag = flip(rows_far, "tensor", 1)

    active = expert_rows((rows_in, rows_core, rows_far, rows_diag), whole)
    active = active.reshape(expert_count, places, columns)
    returned = lax.all_to_all(active, "expert", split_axis=0, concat_axis=0, tiled=True)
    returned = returned.reshape(EXPERTS, step_count, slot_count, columns)
    expert_out = jnp.einsum(
        "sbec,escf->sbf", combine, returned, preferred_element_type=jnp.float32
    ).astype(jnp.bfloat16)
    return (first_new, second_new, attention_out, expert_out)


def solution(mesh):
    return jax.shard_map(
        local,
        mesh=mesh,
        in_specs=(
            P(None, ("group", "expert"), "tensor"),
            P(None, ("group", "expert"), "tensor"),
            P(None, ("group", "expert"), "tensor"),
            P(None, ("group", "expert"), "tensor"),
            P(None, ("group", "expert", "tensor"), None),
            P(None, ("group", "expert", "tensor"), None),
            P(None, ("group", "expert", "tensor"), None),
            P(("group", "expert", "tensor"), None, None),
            P(("group", "expert", "tensor"), None, None),
            P(None, ("group", "expert", "tensor"), None),
            P(None, ("group", "expert", "tensor"), None),
            P(("group", "expert", "tensor")),
            P(None, ("group", "expert"), None),
            P(),
        ),
        out_specs=(
            P(None, ("group", "expert"), "tensor"),
            P(None, ("group", "expert"), "tensor"),
            P(None, ("group", "expert", "tensor"), None),
            P(None, ("group", "expert"), "tensor"),
        ),
        check_vma=False,
    )
```

```python
import jax
import jax.numpy as jnp
from jax import lax
from jax.experimental import pallas as pl
from jax.experimental.pallas import tpu as pltpu
from jax.sharding import PartitionSpec as P

EXPERTS = 32
HEADS = 32
LAT = 512
ROPE = 64


BETA_ONE = 0.9
BETA_TWO = 0.95
LEARN_RATE = 0.005
WEIGHT_DECAY = 0.1
ADAM_EPS = 1e-08
BIAS_ONE = 1.0 - 0.9**10
BIAS_TWO = 1.0 - 0.95**10
QK_SCALE = 192.0 ** (-0.5)
ROUTE_SCALE = 2.827
NEGATIVE = -1e30


def adamw(weights, gradients, moment_one, moment_two):
    grad_wide = gradients.astype(jnp.float32)
    first_new = BETA_ONE * moment_one + (1.0 - BETA_ONE) * grad_wide
    second_new = BETA_TWO * moment_two + (1.0 - BETA_TWO) * grad_wide * grad_wide
    old_weight = weights.astype(jnp.float32)
    ratio = first_new / BIAS_ONE / (jnp.sqrt(second_new / BIAS_TWO) + ADAM_EPS)
    updated = (old_weight - LEARN_RATE * (ratio + WEIGHT_DECAY * old_weight)).astype(jnp.bfloat16)
    return (first_new, second_new, updated)


def attend(query_latent, query_rope, cache_latent, cache_rope, new_latent, new_rope, lengths):
    step_count, row_count = (query_latent.shape[0], query_latent.shape[1])
    slot_total = cache_latent.shape[1]
    query_lat = query_latent.reshape(step_count, row_count, HEADS, LAT)
    query_pos = query_rope.reshape(step_count, row_count, HEADS, ROPE)
    old_scores = (
        jnp.einsum("srhc,rlc->srhl", query_lat, cache_latent, preferred_element_type=jnp.float32)
        + jnp.einsum("srhp,rpl->srhl", query_pos, cache_rope, preferred_element_type=jnp.float32)
    ) * QK_SCALE
    new_scores = (
        jnp.einsum("srhc,trc->srht", query_lat, new_latent, preferred_element_type=jnp.float32)
        + jnp.einsum("srhp,trp->srht", query_pos, new_rope, preferred_element_type=jnp.float32)
    ) * QK_SCALE
    valid_old = jnp.arange(slot_total, dtype=jnp.int32)[None, :] < lengths[:, None]
    valid_new = jnp.arange(step_count)[None, :] <= jnp.arange(step_count)[:, None]
    old_scores = jnp.where(valid_old[None, :, None, :], old_scores, NEGATIVE)
    new_scores = jnp.where(valid_new[:, None, None, :], new_scores, NEGATIVE)
    peak_score = jnp.maximum(
        jnp.max(old_scores, -1, keepdims=True), jnp.max(new_scores, -1, keepdims=True)
    )
    old_mass = jnp.exp(old_scores - peak_score)
    new_mass = jnp.exp(new_scores - peak_score)
    total_mass = jnp.sum(old_mass, -1, keepdims=True) + jnp.sum(new_mass, -1, keepdims=True)
    old_prob = (old_mass / total_mass).astype(jnp.bfloat16)
    new_prob = (new_mass / total_mass).astype(jnp.bfloat16)
    mixture = jnp.einsum(
        "srhl,rlc->srhc", old_prob, cache_latent, preferred_element_type=jnp.float32
    ) + jnp.einsum("srht,trc->srhc", new_prob, new_latent, preferred_element_type=jnp.float32)
    summary = jnp.mean(mixture, 2)
    summary = summary * lax.rsqrt(jnp.mean(summary * summary, -1, keepdims=True) + 1e-05)
    attention_out = mixture.reshape(step_count, row_count, HEADS * LAT).astype(jnp.bfloat16)
    return (attention_out, summary.astype(jnp.bfloat16))


def flip(value, axis, distance):
    size = lax.axis_size(axis)
    return lax.ppermute(value, axis, [(i, i ^ distance) for i in range(size)])


def expert_kernel(turn, own, core, far, diag, whole, out, last, arrival):
    fetch = pltpu.make_async_copy(diag, last, arrival)
    fetch.start()
    total = jnp.dot(own[...], whole[turn[0]], preferred_element_type=jnp.float32)
    for index, part in ((1, core), (2, far), (3, last)):
        if index == 3:
            fetch.wait()
        total = total + jnp.dot(
            part[...],
            whole[jnp.bitwise_xor(turn[0], index)],
            preferred_element_type=jnp.float32,
        )
    out[...] = (total / (1.0 + jnp.exp(-total))).astype(out.dtype)


def expert_rows(parts, whole):
    rows, quarter = parts[0].shape
    columns = whole.shape[2]
    return pl.pallas_call(
        expert_kernel,
        out_shape=jax.ShapeDtypeStruct((rows, columns), jnp.bfloat16),
        in_specs=[pl.BlockSpec(memory_space=pltpu.SMEM)]
        + [pl.BlockSpec(memory_space=pltpu.VMEM)] * 3
        + [pl.BlockSpec(memory_space=pl.ANY), pl.BlockSpec(memory_space=pltpu.VMEM)],
        out_specs=pl.BlockSpec(memory_space=pltpu.VMEM),
        scratch_shapes=[pltpu.VMEM((rows, quarter), jnp.bfloat16), pltpu.SemaphoreType.DMA],
        compiler_params=pltpu.CompilerParams(vmem_limit_bytes=16 * 2**20),
        cost_estimate=pl.CostEstimate(
            flops=8 * rows * quarter * columns,
            bytes_accessed=8 * quarter * (rows + columns),
            transcendentals=rows * columns,
        ),
    )(lax.axis_index("tensor").reshape(1).astype(jnp.int32), *parts, whole)


def local(
    weights,
    gradients,
    moment_one,
    moment_two,
    hidden_in,
    query_latent,
    query_rope,
    cache_latent,
    cache_rope,
    new_latent,
    new_rope,
    lengths,
    expert_ids,
    router,
):
    expert_count, slab, columns = weights.shape
    step_count, _, width = hidden_in.shape
    quarter = width // 4
    my_part = lax.all_to_all(
        jnp.swapaxes(hidden_in.reshape(step_count, 4, quarter), 0, 1),
        "tensor",
        split_axis=0,
        concat_axis=0,
        tiled=True,
    )
    slot_count = 2
    places = step_count * slot_count

    picked = (expert_ids[..., None] == jnp.arange(EXPERTS, dtype=jnp.int32)).astype(jnp.float32)
    per_expert = jnp.sum(picked, 2)
    earlier = jnp.cumsum(per_expert, 1) - per_expert
    slot_hit = (earlier[..., None] == jnp.arange(slot_count, dtype=jnp.float32)).astype(
        jnp.float32
    ) * per_expert[..., None]
    same_step = jnp.eye(step_count, dtype=jnp.float32)
    placed = jnp.transpose(slot_hit, (1, 0, 2, 3))[:, :, :, None] * same_step[:, None, :, None]
    placed = placed.reshape(4 * step_count, expert_count * places).astype(jnp.bfloat16)
    placed, weights = lax.optimization_barrier((placed, weights))
    updated = adamw(weights, gradients, moment_one, moment_two)[2]
    outgoing = lax.dot_general(
        placed,
        my_part.reshape(4 * step_count, quarter),
        (((0,), (0,)), ((), ())),
        preferred_element_type=jnp.float32,
    ).astype(jnp.bfloat16)
    lanes = quarter // 128
    outgoing = jnp.swapaxes(outgoing.reshape(expert_count, places, lanes, 128), 1, 2)
    outgoing = outgoing.reshape(expert_count, places * lanes, 128)
    slabs = jnp.swapaxes(updated.reshape(expert_count, slab, 2, 128), 1, 2)
    slabs = slabs.reshape(expert_count, 2 * slab, 128)
    later = (query_latent, query_rope, cache_rope, new_latent, new_rope, lengths)
    later = later + (gradients, moment_one, moment_two)
    outgoing, later = lax.optimization_barrier((outgoing, later))
    query_latent, query_rope, cache_rope, new_latent, new_rope, lengths = later[:6]
    gradients, moment_one, moment_two = later[6:]
    payload = jnp.concatenate([slabs, outgoing], 1)
    first_new, second_new, _ = adamw(weights, gradients, moment_one, moment_two)
    attention_out, summary = attend(
        query_latent, query_rope, cache_latent, cache_rope, new_latent, new_rope, lengths
    )
    arrived = lax.all_to_all(payload, "expert", split_axis=0, concat_axis=0, tiled=True)
    summary_all = lax.all_gather(summary, "tensor", axis=1, tiled=True)
    logits = jnp.einsum("sbc,ce->sbe", summary_all, router, preferred_element_type=jnp.float32)
    gate_prob = jax.nn.sigmoid(logits)
    chosen = jnp.sum(picked * gate_prob[:, :, None, :], -1)
    route_weight = (ROUTE_SCALE * chosen / jnp.sum(chosen, -1, keepdims=True)).astype(jnp.bfloat16)
    expert_weight = jnp.sum(picked * route_weight.astype(jnp.float32)[..., None], 2)
    combine = (slot_hit * expert_weight[..., None]).astype(jnp.bfloat16)

    held = jnp.swapaxes(arrived[:, : 2 * slab].reshape(expert_count, 2, slab, 128), 1, 2)
    held = held.reshape(expert_count * slab, columns)
    held, combine, first_new, second_new, attention_out = lax.optimization_barrier(
        (held, combine, first_new, second_new, attention_out)
    )
    rows_in = arrived[:, 2 * slab :].reshape(expert_count, lanes, places, 128)
    rows_in = jnp.swapaxes(rows_in, 1, 2).reshape(expert_count * places, quarter)

    copies = jnp.broadcast_to(held[None], (lax.axis_size("group"),) + held.shape)
    whole = lax.all_to_all(copies, "group", split_axis=0, concat_axis=0, tiled=True)
    rows_far = flip(rows_in, "tensor", 2)
    rows_core = flip(rows_in, "tensor", 1)
    rows_diag = flip(rows_far, "tensor", 1)

    active = expert_rows((rows_in, rows_core, rows_far, rows_diag), whole)
    active = active.reshape(expert_count, places, columns)
    returned = lax.all_to_all(active, "expert", split_axis=0, concat_axis=0, tiled=True)
    returned = returned.reshape(EXPERTS, step_count, slot_count, columns)
    expert_out = jnp.einsum(
        "sbec,escf->sbf", combine, returned, preferred_element_type=jnp.float32
    ).astype(jnp.bfloat16)
    return (first_new, second_new, attention_out, expert_out)


def solution(mesh):
    return jax.shard_map(
        local,
        mesh=mesh,
        in_specs=(
            P(None, ("group", "expert"), "tensor"),
            P(None, ("group", "expert"), "tensor"),
            P(None, ("group", "expert"), "tensor"),
            P(None, ("group", "expert"), "tensor"),
            P(None, ("group", "expert", "tensor"), None),
            P(None, ("group", "expert", "tensor"), None),
            P(None, ("group", "expert", "tensor"), None),
            P(("group", "expert", "tensor"), None, None),
            P(("group", "expert", "tensor"), None, None),
            P(None, ("group", "expert", "tensor"), None),
            P(None, ("group", "expert", "tensor"), None),
            P(("group", "expert", "tensor")),
            P(None, ("group", "expert"), None),
            P(),
        ),
        out_specs=(
            P(None, ("group", "expert"), "tensor"),
            P(None, ("group", "expert"), "tensor"),
            P(None, ("group", "expert", "tensor"), None),
            P(None, ("group", "expert"), "tensor"),
        ),
        check_vma=False,
    )
```

```python
import jax
import jax.numpy as jnp
from jax import lax
from jax.experimental import pallas as pl
from jax.experimental.pallas import tpu as pltpu
from jax.sharding import PartitionSpec as P

EXPERTS = 32
HEADS = 32
LAT = 512
ROPE = 64


BETA_ONE = 0.9
BETA_TWO = 0.95
LEARN_RATE = 0.005
WEIGHT_DECAY = 0.1
ADAM_EPS = 1e-08
BIAS_ONE = 1.0 - 0.9**10
BIAS_TWO = 1.0 - 0.95**10
QK_SCALE = 192.0 ** (-0.5)
ROUTE_SCALE = 2.827
NEGATIVE = -1e30


def adamw(weights, gradients, moment_one, moment_two):
    grad_wide = gradients.astype(jnp.float32)
    first_new = BETA_ONE * moment_one + (1.0 - BETA_ONE) * grad_wide
    second_new = BETA_TWO * moment_two + (1.0 - BETA_TWO) * grad_wide * grad_wide
    old_weight = weights.astype(jnp.float32)
    ratio = first_new / BIAS_ONE / (jnp.sqrt(second_new / BIAS_TWO) + ADAM_EPS)
    updated = (old_weight - LEARN_RATE * (ratio + WEIGHT_DECAY * old_weight)).astype(jnp.bfloat16)
    return (first_new, second_new, updated)


def attend(query_latent, query_rope, cache_latent, cache_rope, new_latent, new_rope, lengths):
    step_count, row_count = (query_latent.shape[0], query_latent.shape[1])
    slot_total = cache_latent.shape[1]
    query_lat = query_latent.reshape(step_count, row_count, HEADS, LAT)
    query_pos = query_rope.reshape(step_count, row_count, HEADS, ROPE)
    old_scores = (
        jnp.einsum("srhc,rlc->srhl", query_lat, cache_latent, preferred_element_type=jnp.float32)
        + jnp.einsum("srhp,rpl->srhl", query_pos, cache_rope, preferred_element_type=jnp.float32)
    ) * QK_SCALE
    new_scores = (
        jnp.einsum("srhc,trc->srht", query_lat, new_latent, preferred_element_type=jnp.float32)
        + jnp.einsum("srhp,trp->srht", query_pos, new_rope, preferred_element_type=jnp.float32)
    ) * QK_SCALE
    valid_old = jnp.arange(slot_total, dtype=jnp.int32)[None, :] < lengths[:, None]
    place = lengths[0] + jnp.arange(step_count, dtype=jnp.int32)
    valid_new = place[None, :] <= place[:, None]
    old_scores = jnp.where(valid_old[None, :, None, :], old_scores, NEGATIVE)
    new_scores = jnp.where(valid_new[:, None, None, :], new_scores, NEGATIVE)
    peak_score = jnp.maximum(
        jnp.max(old_scores, -1, keepdims=True), jnp.max(new_scores, -1, keepdims=True)
    )
    old_mass = jnp.exp(old_scores - peak_score)
    new_mass = jnp.exp(new_scores - peak_score)
    total_mass = jnp.sum(old_mass, -1, keepdims=True) + jnp.sum(new_mass, -1, keepdims=True)
    old_prob = (old_mass / total_mass).astype(jnp.bfloat16)
    new_prob = (new_mass / total_mass).astype(jnp.bfloat16)
    mixture = jnp.einsum(
        "srhl,rlc->srhc", old_prob, cache_latent, preferred_element_type=jnp.float32
    ) + jnp.einsum("srht,trc->srhc", new_prob, new_latent, preferred_element_type=jnp.float32)
    summary = jnp.mean(mixture, 2)
    summary = summary * lax.rsqrt(jnp.mean(summary * summary, -1, keepdims=True) + 1e-05)
    attention_out = mixture.reshape(step_count, row_count, HEADS * LAT).astype(jnp.bfloat16)
    return (attention_out, summary.astype(jnp.bfloat16))


def flip(value, axis, distance):
    size = lax.axis_size(axis)
    return lax.ppermute(value, axis, [(i, i ^ distance) for i in range(size)])


def expert_kernel(turn, own, core, far, diag, whole, out, last, arrival):
    fetch = pltpu.make_async_copy(diag, last, arrival)
    fetch.start()
    total = jnp.dot(own[...], whole[turn[0]], preferred_element_type=jnp.float32)
    for index, part in ((1, core), (2, far), (3, last)):
        if index == 3:
            fetch.wait()
        total = total + jnp.dot(
            part[...],
            whole[jnp.bitwise_xor(turn[0], index)],
            preferred_element_type=jnp.float32,
        )
    out[...] = (total / (1.0 + jnp.exp(-total))).astype(out.dtype)


def expert_rows(parts, whole):
    rows, quarter = parts[0].shape
    columns = whole.shape[2]
    return pl.pallas_call(
        expert_kernel,
        out_shape=jax.ShapeDtypeStruct((rows, columns), jnp.bfloat16),
        in_specs=[pl.BlockSpec(memory_space=pltpu.SMEM)]
        + [pl.BlockSpec(memory_space=pltpu.VMEM)] * 3
        + [pl.BlockSpec(memory_space=pl.ANY), pl.BlockSpec(memory_space=pltpu.VMEM)],
        out_specs=pl.BlockSpec(memory_space=pltpu.VMEM),
        scratch_shapes=[pltpu.VMEM((rows, quarter), jnp.bfloat16), pltpu.SemaphoreType.DMA],
        compiler_params=pltpu.CompilerParams(vmem_limit_bytes=16 * 2**20),
        cost_estimate=pl.CostEstimate(
            flops=8 * rows * quarter * columns,
            bytes_accessed=8 * quarter * (rows + columns),
            transcendentals=rows * columns,
        ),
    )(lax.axis_index("tensor").reshape(1).astype(jnp.int32), *parts, whole)


def local(
    weights,
    gradients,
    moment_one,
    moment_two,
    hidden_in,
    query_latent,
    query_rope,
    cache_latent,
    cache_rope,
    new_latent,
    new_rope,
    lengths,
    expert_ids,
    router,
):
    expert_count, slab, columns = weights.shape
    step_count, _, width = hidden_in.shape
    quarter = width // 4
    my_part = lax.all_to_all(
        jnp.swapaxes(hidden_in.reshape(step_count, 4, quarter), 0, 1),
        "tensor",
        split_axis=0,
        concat_axis=0,
        tiled=True,
    )
    slot_count = 2
    places = step_count * slot_count

    picked = (expert_ids[..., None] == jnp.arange(EXPERTS, dtype=jnp.int32)).astype(jnp.float32)
    per_expert = jnp.sum(picked, 2)
    earlier = jnp.cumsum(per_expert, 1) - per_expert
    slot_hit = (earlier[..., None] == jnp.arange(slot_count, dtype=jnp.float32)).astype(
        jnp.float32
    ) * per_expert[..., None]
    same_step = jnp.eye(step_count, dtype=jnp.float32)
    placed = jnp.transpose(slot_hit, (1, 0, 2, 3))[:, :, :, None] * same_step[:, None, :, None]
    placed = placed.reshape(4 * step_count, expert_count * places).astype(jnp.bfloat16)
    placed, weights = lax.optimization_barrier((placed, weights))
    updated = adamw(weights, gradients, moment_one, moment_two)[2]
    outgoing = lax.dot_general(
        placed,
        my_part.reshape(4 * step_count, quarter),
        (((0,), (0,)), ((), ())),
        preferred_element_type=jnp.float32,
    ).astype(jnp.bfloat16)
    lanes = quarter // 128
    outgoing = jnp.swapaxes(outgoing.reshape(expert_count, places, lanes, 128), 1, 2)
    outgoing = outgoing.reshape(expert_count, places * lanes, 128)
    slabs = jnp.swapaxes(updated.reshape(expert_count, slab, 2, 128), 1, 2)
    slabs = slabs.reshape(expert_count, 2 * slab, 128)
    later = (query_latent, query_rope, cache_rope, new_latent, new_rope, lengths)
    later = later + (gradients, moment_one, moment_two)
    outgoing, slabs, later = lax.optimization_barrier((outgoing, slabs, later))
    query_latent, query_rope, cache_rope, new_latent, new_rope, lengths = later[:6]
    gradients, moment_one, moment_two = later[6:]
    payload = jnp.concatenate([slabs, outgoing], 1)
    first_new, second_new, _ = adamw(weights, gradients, moment_one, moment_two)
    attention_out, summary = attend(
        query_latent, query_rope, cache_latent, cache_rope, new_latent, new_rope, lengths
    )
    arrived = lax.all_to_all(payload, "expert", split_axis=0, concat_axis=0, tiled=True)
    summary_all = lax.all_gather(summary, "tensor", axis=1, tiled=True)
    logits = jnp.einsum("sbc,ce->sbe", summary_all, router, preferred_element_type=jnp.float32)
    gate_prob = jax.nn.sigmoid(logits)
    chosen = jnp.sum(picked * gate_prob[:, :, None, :], -1)
    route_weight = (ROUTE_SCALE * chosen / jnp.sum(chosen, -1, keepdims=True)).astype(jnp.bfloat16)
    expert_weight = jnp.sum(picked * route_weight.astype(jnp.float32)[..., None], 2)
    combine = (slot_hit * expert_weight[..., None]).astype(jnp.bfloat16)

    held = jnp.swapaxes(arrived[:, : 2 * slab].reshape(expert_count, 2, slab, 128), 1, 2)
    held = held.reshape(expert_count * slab, columns)
    held, combine, first_new, second_new, attention_out = lax.optimization_barrier(
        (held, combine, first_new, second_new, attention_out)
    )
    rows_in = arrived[:, 2 * slab :].reshape(expert_count, lanes, places, 128)
    rows_in = jnp.swapaxes(rows_in, 1, 2).reshape(expert_count * places, quarter)

    copies = jnp.broadcast_to(held[None], (lax.axis_size("group"),) + held.shape)
    whole = lax.all_to_all(copies, "group", split_axis=0, concat_axis=0, tiled=True)
    rows_far = flip(rows_in, "tensor", 2)
    rows_core = flip(rows_in, "tensor", 1)
    rows_diag = flip(rows_far, "tensor", 1)

    active = expert_rows((rows_in, rows_core, rows_far, rows_diag), whole)
    active = active.reshape(expert_count, places, columns)
    returned = lax.all_to_all(active, "expert", split_axis=0, concat_axis=0, tiled=True)
    returned = returned.reshape(EXPERTS, step_count, slot_count, columns)
    expert_out = jnp.einsum(
        "sbec,escf->sbf", combine, returned, preferred_element_type=jnp.float32
    ).astype(jnp.bfloat16)
    return (first_new, second_new, attention_out, expert_out)


def solution(mesh):
    return jax.shard_map(
        local,
        mesh=mesh,
        in_specs=(
            P(None, ("group", "expert"), "tensor"),
            P(None, ("group", "expert"), "tensor"),
            P(None, ("group", "expert"), "tensor"),
            P(None, ("group", "expert"), "tensor"),
            P(None, ("group", "expert", "tensor"), None),
            P(None, ("group", "expert", "tensor"), None),
            P(None, ("group", "expert", "tensor"), None),
            P(("group", "expert", "tensor"), None, None),
            P(("group", "expert", "tensor"), None, None),
            P(None, ("group", "expert", "tensor"), None),
            P(None, ("group", "expert", "tensor"), None),
            P(("group", "expert", "tensor")),
            P(None, ("group", "expert"), None),
            P(),
        ),
        out_specs=(
            P(None, ("group", "expert"), "tensor"),
            P(None, ("group", "expert"), "tensor"),
            P(None, ("group", "expert", "tensor"), None),
            P(None, ("group", "expert"), "tensor"),
        ),
        check_vma=False,
    )
```

```python
import jax
import jax.numpy as jnp
import numpy as np
from jax import lax
from jax.experimental import pallas as pl
from jax.experimental.pallas import tpu as pltpu
from jax.sharding import PartitionSpec as P

EXPERTS = 32
HEADS = 32
LAT = 512
ROPE = 64


BETA_ONE = 0.9
BETA_TWO = 0.95
LEARN_RATE = 0.005
WEIGHT_DECAY = 0.1
ADAM_EPS = 1e-08
BIAS_ONE = 1.0 - 0.9**10
BIAS_TWO = 1.0 - 0.95**10
QK_SCALE = 192.0 ** (-0.5)
ROUTE_SCALE = 2.827
NEGATIVE = -1e30


def adamw(weights, gradients, moment_one, moment_two):
    grad_wide = gradients.astype(jnp.float32)
    first_new = BETA_ONE * moment_one + (1.0 - BETA_ONE) * grad_wide
    second_new = BETA_TWO * moment_two + (1.0 - BETA_TWO) * grad_wide * grad_wide
    old_weight = weights.astype(jnp.float32)
    ratio = first_new / BIAS_ONE / (jnp.sqrt(second_new / BIAS_TWO) + ADAM_EPS)
    updated = (old_weight - LEARN_RATE * (ratio + WEIGHT_DECAY * old_weight)).astype(jnp.bfloat16)
    return (first_new, second_new, updated)


def attend(query_latent, query_rope, cache_latent, cache_rope, new_latent, new_rope, lengths):
    step_count, row_count = (query_latent.shape[0], query_latent.shape[1])
    slot_total = cache_latent.shape[1]
    query_lat = query_latent.reshape(step_count, row_count, HEADS, LAT)
    query_pos = query_rope.reshape(step_count, row_count, HEADS, ROPE)
    old_scores = (
        jnp.einsum("srhc,rlc->srhl", query_lat, cache_latent, preferred_element_type=jnp.float32)
        + jnp.einsum("srhp,rpl->srhl", query_pos, cache_rope, preferred_element_type=jnp.float32)
    ) * QK_SCALE
    new_scores = (
        jnp.einsum("srhc,trc->srht", query_lat, new_latent, preferred_element_type=jnp.float32)
        + jnp.einsum("srhp,trp->srht", query_pos, new_rope, preferred_element_type=jnp.float32)
    ) * QK_SCALE
    valid_old = jnp.arange(slot_total, dtype=jnp.int32)[None, :] < lengths[:, None]
    valid_new = np.arange(step_count)[None, :] <= np.arange(step_count)[:, None]
    old_scores = jnp.where(valid_old[None, :, None, :], old_scores, NEGATIVE)
    new_scores = jnp.where(jnp.asarray(valid_new[:, None, None, :]), new_scores, NEGATIVE)
    peak_score = jnp.maximum(
        jnp.max(old_scores, -1, keepdims=True), jnp.max(new_scores, -1, keepdims=True)
    )
    old_mass = jnp.exp(old_scores - peak_score)
    new_mass = jnp.exp(new_scores - peak_score)
    total_mass = jnp.sum(old_mass, -1, keepdims=True) + jnp.sum(new_mass, -1, keepdims=True)
    old_prob = (old_mass / total_mass).astype(jnp.bfloat16)
    new_prob = (new_mass / total_mass).astype(jnp.bfloat16)
    mixture = jnp.einsum(
        "srhl,rlc->srhc", old_prob, cache_latent, preferred_element_type=jnp.float32
    ) + jnp.einsum("srht,trc->srhc", new_prob, new_latent, preferred_element_type=jnp.float32)
    summary = jnp.mean(mixture, 2)
    summary = summary * lax.rsqrt(jnp.mean(summary * summary, -1, keepdims=True) + 1e-05)
    attention_out = mixture.reshape(step_count, row_count, HEADS * LAT).astype(jnp.bfloat16)
    return (attention_out, summary.astype(jnp.bfloat16))


def flip(value, axis, distance):
    size = lax.axis_size(axis)
    return lax.ppermute(value, axis, [(i, i ^ distance) for i in range(size)])


def expert_kernel(turn, own, core, far, diag, whole, out, last, arrival):
    fetch = pltpu.make_async_copy(diag, last, arrival)
    fetch.start()
    total = jnp.dot(own[...], whole[turn[0]], preferred_element_type=jnp.float32)
    for index, part in ((1, core), (2, far), (3, last)):
        if index == 3:
            fetch.wait()
        total = total + jnp.dot(
            part[...],
            whole[jnp.bitwise_xor(turn[0], index)],
            preferred_element_type=jnp.float32,
        )
    out[...] = (total / (1.0 + jnp.exp(-total))).astype(out.dtype)


def expert_rows(parts, whole):
    rows, quarter = parts[0].shape
    columns = whole.shape[2]
    return pl.pallas_call(
        expert_kernel,
        out_shape=jax.ShapeDtypeStruct((rows, columns), jnp.bfloat16),
        in_specs=[pl.BlockSpec(memory_space=pltpu.SMEM)]
        + [pl.BlockSpec(memory_space=pltpu.VMEM)] * 3
        + [pl.BlockSpec(memory_space=pl.ANY), pl.BlockSpec(memory_space=pltpu.VMEM)],
        out_specs=pl.BlockSpec(memory_space=pltpu.VMEM),
        scratch_shapes=[pltpu.VMEM((rows, quarter), jnp.bfloat16), pltpu.SemaphoreType.DMA],
        compiler_params=pltpu.CompilerParams(vmem_limit_bytes=16 * 2**20),
        cost_estimate=pl.CostEstimate(
            flops=8 * rows * quarter * columns,
            bytes_accessed=8 * quarter * (rows + columns),
            transcendentals=rows * columns,
        ),
    )(lax.axis_index("tensor").reshape(1).astype(jnp.int32), *parts, whole)


def local(
    weights,
    gradients,
    moment_one,
    moment_two,
    hidden_in,
    query_latent,
    query_rope,
    cache_latent,
    cache_rope,
    new_latent,
    new_rope,
    lengths,
    expert_ids,
    router,
):
    expert_count, slab, columns = weights.shape
    step_count, _, width = hidden_in.shape
    quarter = width // 4
    my_part = lax.all_to_all(
        jnp.swapaxes(hidden_in.reshape(step_count, 4, quarter), 0, 1),
        "tensor",
        split_axis=0,
        concat_axis=0,
        tiled=True,
    )
    slot_count = 2
    places = step_count * slot_count

    picked = (expert_ids[..., None] == jnp.arange(EXPERTS, dtype=jnp.int32)).astype(jnp.float32)
    per_expert = jnp.sum(picked, 2)
    earlier = jnp.cumsum(per_expert, 1) - per_expert
    slot_hit = (earlier[..., None] == jnp.arange(slot_count, dtype=jnp.float32)).astype(
        jnp.float32
    ) * per_expert[..., None]
    same_step = jnp.eye(step_count, dtype=jnp.float32)
    placed = jnp.transpose(slot_hit, (1, 0, 2, 3))[:, :, :, None] * same_step[:, None, :, None]
    placed = placed.reshape(4 * step_count, expert_count * places).astype(jnp.bfloat16)
    placed, weights = lax.optimization_barrier((placed, weights))
    updated = adamw(weights, gradients, moment_one, moment_two)[2]
    outgoing = lax.dot_general(
        placed,
        my_part.reshape(4 * step_count, quarter),
        (((0,), (0,)), ((), ())),
        preferred_element_type=jnp.float32,
    ).astype(jnp.bfloat16)
    lanes = quarter // 128
    outgoing = jnp.swapaxes(outgoing.reshape(expert_count, places, lanes, 128), 1, 2)
    outgoing = outgoing.reshape(expert_count, places * lanes, 128)
    slabs = jnp.swapaxes(updated.reshape(expert_count, slab, 2, 128), 1, 2)
    slabs = slabs.reshape(expert_count, 2 * slab, 128)
    later = (query_latent, query_rope, cache_rope, new_latent, new_rope, lengths)
    later = later + (gradients, moment_one, moment_two)
    outgoing, later = lax.optimization_barrier((outgoing, later))
    query_latent, query_rope, cache_rope, new_latent, new_rope, lengths = later[:6]
    gradients, moment_one, moment_two = later[6:]
    payload = jnp.concatenate([slabs, outgoing], 1)
    first_new, second_new, _ = adamw(weights, gradients, moment_one, moment_two)
    attention_out, summary = attend(
        query_latent, query_rope, cache_latent, cache_rope, new_latent, new_rope, lengths
    )
    arrived = lax.all_to_all(payload, "expert", split_axis=0, concat_axis=0, tiled=True)
    summary_all = lax.all_gather(summary, "tensor", axis=1, tiled=True)
    logits = jnp.einsum("sbc,ce->sbe", summary_all, router, preferred_element_type=jnp.float32)
    gate_prob = jax.nn.sigmoid(logits)
    chosen = jnp.sum(picked * gate_prob[:, :, None, :], -1)
    route_weight = (ROUTE_SCALE * chosen / jnp.sum(chosen, -1, keepdims=True)).astype(jnp.bfloat16)
    expert_weight = jnp.sum(picked * route_weight.astype(jnp.float32)[..., None], 2)
    combine = (slot_hit * expert_weight[..., None]).astype(jnp.bfloat16)

    held = jnp.swapaxes(arrived[:, : 2 * slab].reshape(expert_count, 2, slab, 128), 1, 2)
    held = held.reshape(expert_count * slab, columns)
    held, combine, first_new, second_new, attention_out = lax.optimization_barrier(
        (held, combine, first_new, second_new, attention_out)
    )
    rows_in = arrived[:, 2 * slab :].reshape(expert_count, lanes, places, 128)
    rows_in = jnp.swapaxes(rows_in, 1, 2).reshape(expert_count * places, quarter)

    copies = jnp.broadcast_to(held[None], (lax.axis_size("group"),) + held.shape)
    whole = lax.all_to_all(copies, "group", split_axis=0, concat_axis=0, tiled=True)
    rows_far = flip(rows_in, "tensor", 2)
    rows_core = flip(rows_in, "tensor", 1)
    rows_diag = flip(rows_far, "tensor", 1)

    active = expert_rows((rows_in, rows_core, rows_far, rows_diag), whole)
    active = active.reshape(expert_count, places, columns)
    returned = lax.all_to_all(active, "expert", split_axis=0, concat_axis=0, tiled=True)
    returned = returned.reshape(EXPERTS, step_count, slot_count, columns)
    expert_out = jnp.einsum(
        "sbec,escf->sbf", combine, returned, preferred_element_type=jnp.float32
    ).astype(jnp.bfloat16)
    return (first_new, second_new, attention_out, expert_out)


def solution(mesh):
    return jax.shard_map(
        local,
        mesh=mesh,
        in_specs=(
            P(None, ("group", "expert"), "tensor"),
            P(None, ("group", "expert"), "tensor"),
            P(None, ("group", "expert"), "tensor"),
            P(None, ("group", "expert"), "tensor"),
            P(None, ("group", "expert", "tensor"), None),
            P(None, ("group", "expert", "tensor"), None),
            P(None, ("group", "expert", "tensor"), None),
            P(("group", "expert", "tensor"), None, None),
            P(("group", "expert", "tensor"), None, None),
            P(None, ("group", "expert", "tensor"), None),
            P(None, ("group", "expert", "tensor"), None),
            P(("group", "expert", "tensor")),
            P(None, ("group", "expert"), None),
            P(),
        ),
        out_specs=(
            P(None, ("group", "expert"), "tensor"),
            P(None, ("group", "expert"), "tensor"),
            P(None, ("group", "expert", "tensor"), None),
            P(None, ("group", "expert"), "tensor"),
        ),
        check_vma=False,
    )
```

```python
import jax
import jax.numpy as jnp
import numpy as np
from jax import lax
from jax.experimental import pallas as pl
from jax.experimental.pallas import tpu as pltpu
from jax.sharding import PartitionSpec as P

EXPERTS = 32
HEADS = 32
LAT = 512
ROPE = 64


BETA_ONE = 0.9
BETA_TWO = 0.95
LEARN_RATE = 0.005
WEIGHT_DECAY = 0.1
ADAM_EPS = 1e-08
BIAS_ONE = 1.0 - 0.9**10
BIAS_TWO = 1.0 - 0.95**10
QK_SCALE = 192.0 ** (-0.5)
ROUTE_SCALE = 2.827
NEGATIVE = -1e30


def adamw(weights, gradients, moment_one, moment_two):
    grad_wide = gradients.astype(jnp.float32)
    first_new = BETA_ONE * moment_one + (1.0 - BETA_ONE) * grad_wide
    second_new = BETA_TWO * moment_two + (1.0 - BETA_TWO) * grad_wide * grad_wide
    old_weight = weights.astype(jnp.float32)
    ratio = first_new / BIAS_ONE / (jnp.sqrt(second_new / BIAS_TWO) + ADAM_EPS)
    updated = (old_weight - LEARN_RATE * (ratio + WEIGHT_DECAY * old_weight)).astype(jnp.bfloat16)
    return (first_new, second_new, updated)


def attend(query_latent, query_rope, cache_latent, cache_rope, new_latent, new_rope, lengths):
    step_count, row_count = (query_latent.shape[0], query_latent.shape[1])
    slot_total = cache_latent.shape[1]
    query_lat = query_latent.reshape(step_count, row_count, HEADS, LAT)
    query_pos = query_rope.reshape(step_count, row_count, HEADS, ROPE)
    old_scores = (
        jnp.einsum("srhc,rlc->srhl", query_lat, cache_latent, preferred_element_type=jnp.float32)
        + jnp.einsum("srhp,rpl->srhl", query_pos, cache_rope, preferred_element_type=jnp.float32)
    ) * QK_SCALE
    new_scores = (
        jnp.einsum("srhc,trc->srht", query_lat, new_latent, preferred_element_type=jnp.float32)
        + jnp.einsum("srhp,trp->srht", query_pos, new_rope, preferred_element_type=jnp.float32)
    ) * QK_SCALE
    valid_old = jnp.arange(slot_total, dtype=jnp.int32)[None, :] < lengths[:, None]
    valid_new = np.arange(step_count)[None, :] <= np.arange(step_count)[:, None]
    old_scores = jnp.where(valid_old[None, :, None, :], old_scores, NEGATIVE)
    new_scores = jnp.where(jnp.asarray(valid_new[:, None, None, :]), new_scores, NEGATIVE)
    peak_score = jnp.maximum(
        jnp.max(old_scores, -1, keepdims=True), jnp.max(new_scores, -1, keepdims=True)
    )
    old_mass = jnp.exp(old_scores - peak_score)
    new_mass = jnp.exp(new_scores - peak_score)
    total_mass = jnp.sum(old_mass, -1, keepdims=True) + jnp.sum(new_mass, -1, keepdims=True)
    old_prob = (old_mass / total_mass).astype(jnp.bfloat16)
    new_prob = (new_mass / total_mass).astype(jnp.bfloat16)
    mixture = jnp.einsum(
        "srhl,rlc->srhc", old_prob, cache_latent, preferred_element_type=jnp.float32
    ) + jnp.einsum("srht,trc->srhc", new_prob, new_latent, preferred_element_type=jnp.float32)
    summary = jnp.mean(mixture, 2)
    summary = summary * lax.rsqrt(jnp.mean(summary * summary, -1, keepdims=True) + 1e-05)
    attention_out = mixture.reshape(step_count, row_count, HEADS * LAT).astype(jnp.bfloat16)
    return (attention_out, summary.astype(jnp.bfloat16))


def place_rows(expert_ids, slot_count):
    picked = (expert_ids[..., None] == jnp.arange(EXPERTS, dtype=jnp.int32)).astype(jnp.float32)
    per_expert = jnp.sum(picked, 2)
    earlier = jnp.cumsum(per_expert, 1) - per_expert
    slot_hit = (earlier[..., None] == jnp.arange(slot_count, dtype=jnp.float32)).astype(
        jnp.float32
    ) * per_expert[..., None]
    return picked, slot_hit


def flip(value, axis, distance):
    size = lax.axis_size(axis)
    return lax.ppermute(value, axis, [(i, i ^ distance) for i in range(size)])


def expert_kernel(turn, own, core, far, diag, whole, out, last, arrival):
    fetch = pltpu.make_async_copy(diag, last, arrival)
    fetch.start()
    total = jnp.dot(own[...], whole[turn[0]], preferred_element_type=jnp.float32)
    for index, part in ((1, core), (2, far), (3, last)):
        if index == 3:
            fetch.wait()
        total = total + jnp.dot(
            part[...],
            whole[jnp.bitwise_xor(turn[0], index)],
            preferred_element_type=jnp.float32,
        )
    out[...] = (total / (1.0 + jnp.exp(-total))).astype(out.dtype)


def expert_rows(parts, whole):
    rows, quarter = parts[0].shape
    columns = whole.shape[2]
    return pl.pallas_call(
        expert_kernel,
        out_shape=jax.ShapeDtypeStruct((rows, columns), jnp.bfloat16),
        in_specs=[pl.BlockSpec(memory_space=pltpu.SMEM)]
        + [pl.BlockSpec(memory_space=pltpu.VMEM)] * 3
        + [pl.BlockSpec(memory_space=pl.ANY), pl.BlockSpec(memory_space=pltpu.VMEM)],
        out_specs=pl.BlockSpec(memory_space=pltpu.VMEM),
        scratch_shapes=[pltpu.VMEM((rows, quarter), jnp.bfloat16), pltpu.SemaphoreType.DMA],
        compiler_params=pltpu.CompilerParams(vmem_limit_bytes=16 * 2**20),
        cost_estimate=pl.CostEstimate(
            flops=8 * rows * quarter * columns,
            bytes_accessed=8 * quarter * (rows + columns),
            transcendentals=rows * columns,
        ),
    )(lax.axis_index("tensor").reshape(1).astype(jnp.int32), *parts, whole)


def local(
    weights,
    gradients,
    moment_one,
    moment_two,
    hidden_in,
    query_latent,
    query_rope,
    cache_latent,
    cache_rope,
    new_latent,
    new_rope,
    lengths,
    expert_ids,
    router,
):
    expert_count, slab, columns = weights.shape
    step_count, _, width = hidden_in.shape
    quarter = width // 4
    my_part = lax.all_to_all(
        jnp.swapaxes(hidden_in.reshape(step_count, 4, quarter), 0, 1),
        "tensor",
        split_axis=0,
        concat_axis=0,
        tiled=True,
    )
    slot_count = 2
    places = step_count * slot_count

    _, slot_hit = place_rows(expert_ids, slot_count)
    same_step = jnp.eye(step_count, dtype=jnp.float32)
    placed = jnp.transpose(slot_hit, (1, 0, 2, 3))[:, :, :, None] * same_step[:, None, :, None]
    placed = placed.reshape(4 * step_count, expert_count * places).astype(jnp.bfloat16)
    placed, weights = lax.optimization_barrier((placed, weights))
    updated = adamw(weights, gradients, moment_one, moment_two)[2]
    outgoing = lax.dot_general(
        placed,
        my_part.reshape(4 * step_count, quarter),
        (((0,), (0,)), ((), ())),
        preferred_element_type=jnp.float32,
    ).astype(jnp.bfloat16)
    lanes = quarter // 128
    outgoing = jnp.swapaxes(outgoing.reshape(expert_count, places, lanes, 128), 1, 2)
    outgoing = outgoing.reshape(expert_count, places * lanes, 128)
    slabs = jnp.swapaxes(updated.reshape(expert_count, slab, 2, 128), 1, 2)
    slabs = slabs.reshape(expert_count, 2 * slab, 128)
    later = (query_latent, query_rope, cache_rope, new_latent, new_rope, expert_ids)
    later = later + (gradients, moment_one, moment_two)
    outgoing, later = lax.optimization_barrier((outgoing, later))
    query_latent, query_rope, cache_rope, new_latent, new_rope, expert_ids = later[:6]
    gradients, moment_one, moment_two = later[6:]
    payload = jnp.concatenate([slabs, outgoing], 1)
    first_new, second_new, _ = adamw(weights, gradients, moment_one, moment_two)
    attention_out, summary = attend(
        query_latent, query_rope, cache_latent, cache_rope, new_latent, new_rope, lengths
    )
    arrived = lax.all_to_all(payload, "expert", split_axis=0, concat_axis=0, tiled=True)
    summary_all = lax.all_gather(summary, "tensor", axis=1, tiled=True)
    logits = jnp.einsum("sbc,ce->sbe", summary_all, router, preferred_element_type=jnp.float32)
    gate_prob = jax.nn.sigmoid(logits)
    picked, slot_hit = place_rows(expert_ids, slot_count)
    chosen = jnp.sum(picked * gate_prob[:, :, None, :], -1)
    route_weight = (ROUTE_SCALE * chosen / jnp.sum(chosen, -1, keepdims=True)).astype(jnp.bfloat16)
    expert_weight = jnp.sum(picked * route_weight.astype(jnp.float32)[..., None], 2)
    combine = (slot_hit * expert_weight[..., None]).astype(jnp.bfloat16)

    held = jnp.swapaxes(arrived[:, : 2 * slab].reshape(expert_count, 2, slab, 128), 1, 2)
    held = held.reshape(expert_count * slab, columns)
    held, combine, first_new, second_new, attention_out = lax.optimization_barrier(
        (held, combine, first_new, second_new, attention_out)
    )
    rows_in = arrived[:, 2 * slab :].reshape(expert_count, lanes, places, 128)
    rows_in = jnp.swapaxes(rows_in, 1, 2).reshape(expert_count * places, quarter)

    copies = jnp.broadcast_to(held[None], (lax.axis_size("group"),) + held.shape)
    whole = lax.all_to_all(copies, "group", split_axis=0, concat_axis=0, tiled=True)
    rows_far = flip(rows_in, "tensor", 2)
    rows_core = flip(rows_in, "tensor", 1)
    rows_diag = flip(rows_far, "tensor", 1)

    active = expert_rows((rows_in, rows_core, rows_far, rows_diag), whole)
    active = active.reshape(expert_count, places, columns)
    returned = lax.all_to_all(active, "expert", split_axis=0, concat_axis=0, tiled=True)
    returned = returned.reshape(EXPERTS, step_count, slot_count, columns)
    expert_out = jnp.einsum(
        "sbec,escf->sbf", combine, returned, preferred_element_type=jnp.float32
    ).astype(jnp.bfloat16)
    return (first_new, second_new, attention_out, expert_out)


def solution(mesh):
    return jax.shard_map(
        local,
        mesh=mesh,
        in_specs=(
            P(None, ("group", "expert"), "tensor"),
            P(None, ("group", "expert"), "tensor"),
            P(None, ("group", "expert"), "tensor"),
            P(None, ("group", "expert"), "tensor"),
            P(None, ("group", "expert", "tensor"), None),
            P(None, ("group", "expert", "tensor"), None),
            P(None, ("group", "expert", "tensor"), None),
            P(("group", "expert", "tensor"), None, None),
            P(("group", "expert", "tensor"), None, None),
            P(None, ("group", "expert", "tensor"), None),
            P(None, ("group", "expert", "tensor"), None),
            P(("group", "expert", "tensor")),
            P(None, ("group", "expert"), None),
            P(),
        ),
        out_specs=(
            P(None, ("group", "expert"), "tensor"),
            P(None, ("group", "expert"), "tensor"),
            P(None, ("group", "expert", "tensor"), None),
            P(None, ("group", "expert"), "tensor"),
        ),
        check_vma=False,
    )
```
